512 devices in a mesh: row: 16 (over x_hi, y), col: 16 (over z, core), layer: 2 (over x_lo).
Axes of the slice: x: 4 (x_hi: 2, x_lo: 2; x = x_hi * 2 + x_lo), y: 8, z: 8, core: 2. Of those that a mesh axis runs over, the one named last changes fastest.
Arguments:
- a_blocks: float32 [256, 8, 128, 128], P(('row', 'col'), 'layer'), may hold values from -0.1875 to 0.1875
- p_blocks: float32 [256, 8, 128, 128], P(('row', 'col'), 'layer'), may hold values from -6 to 6
- out_columns: int32 [256, 64], P('row', 'col'), may hold values from 0 to 15
- pair_codes: int32 [256, 64, 14], P('row', 'col', 'layer'), may hold values from 0 to 16, as said below
Outputs:
- c_blocks: float32 [256, 64, 128, 128], P(('row', 'layer'), 'col')
The draws below stay inside these ranges and needn't reach their ends.
Inputs may be any that keep to these rules, and one draw needn't show every extreme that they name: `pair_codes`: within each block (r, s) and inner range, the first entries are live and pairwise distinct, all later ones equal 16; at least one is live, and product slot 0 of every block row has all 7 live.
All inputs are finite; a program needn't handle non-finite values.
Results may differ from the reference program's by a relative error of at most 0.0003.
Values sent between devices are 32-bit elements; how exact they have to be, the bound alone decides.
A program may use at most 64 MiB of HBM per device.

```python
import jax
import jax.numpy as jnp
from jax import lax

BS = 128
CB_DEV = 1
NA = 4
NP = 4
OC = 4
MP = 7
CB = 16
MB = 256
NBC = 256
OS_ALL = 64
SA_ALL = 8
SP_ALL = 8
CODES = 14
N_COL = 16
N_LAYER = 2


def draw_pair_codes(key, part):
    key = jax.random.fold_in(key, 7)
    key_order, key_live = jax.random.split(key)
    pair_total = NA * NP
    shape_three = (MB, OS_ALL, N_LAYER)
    scores = jax.random.randint(key_order, shape_three + (pair_total,), 0, 2 ** 20) * pair_total
    scores = scores + jnp.arange(pair_total, dtype=jnp.int32)
    order = jnp.argsort(scores, axis=-1, stable=True)[..., :MP].astype(jnp.int32)
    live_count = jax.random.randint(key_live, shape_three, 1, MP + 1)
    slot_index = jnp.arange(OS_ALL, dtype=jnp.int32)[None, :, None]
    live_count = jnp.where(slot_index == 0, MP, live_count)
    position = jnp.arange(MP, dtype=jnp.int32)
    codes_all = jnp.where(position < live_count[..., None], order, pair_total)
    return codes_all.reshape(MB, OS_ALL, N_LAYER * MP).astype(jnp.int32)


def place_ends(array, stream_key, low, top_value):
    extent = array.shape
    index_at = [jax.random.randint(jax.random.fold_in(stream_key, axis), (), 0, extent[axis]) for axis in range(len(extent))]
    array = array.at[tuple(index_at)].set(low)
    longest = extent.index(max(extent))
    index_at[longest] = (index_at[longest] + 1) % extent[longest]
    return array.at[tuple(index_at)].set(top_value)


def levels(stream_key, extent, pieces, low, largest):
    loudness = 1.0
    for dim, shards_of in pieces:
        draws = jax.random.uniform(jax.random.fold_in(jax.random.fold_in(stream_key, 6), dim), (shards_of,), jnp.float32, low / len(pieces), largest / len(pieces))
        loudness = loudness * jnp.repeat(jnp.exp(draws), extent[dim] // shards_of).reshape((-1,) + (1,) * (len(extent) - 1 - dim))
    return loudness


def noise(stream_key, shape, width, limit, cuts=(), held_as=jnp.bfloat16):
    loudness = levels(stream_key, shape, cuts, -0.22, 0.18) if cuts else 1.0
    values = jax.random.normal(stream_key, shape, jnp.float32) * width * loudness
    return jnp.minimum(jnp.maximum(values, -limit), limit).astype(held_as)


def setup_inputs(seed: int = 0) -> dict:
    arg_keys = jax.random.split(jax.random.key(seed), 5)
    return {
        "a_blocks": noise(arg_keys[0], (MB, SA_ALL, BS, BS), (BS * MP) ** -0.5, 0.1875, ((0, 256), (1, 2)), jnp.float32),
        "p_blocks": noise(arg_keys[1], (NBC, SP_ALL, BS, BS), 1.0, 6.0, ((0, 256), (1, 2)), jnp.float32),
        "out_columns": place_ends(jax.random.randint(arg_keys[2], (MB, OS_ALL), 0, CB), jax.random.fold_in(arg_keys[2], 1), 0, CB - 1).astype(jnp.int32),
        "pair_codes": draw_pair_codes(jax.random.fold_in(arg_keys[4], 71), 0),
    }


def reference(a_blocks, p_blocks, out_columns, pair_codes):
    def one_row(inputs):
        a_row, out_cols, pair_list = inputs
        panel_index = (jnp.arange(OS_ALL) // OC).astype(jnp.int32)
        global_col = ((out_cols // CB_DEV) * N_COL + panel_index) * CB_DEV + out_cols % CB_DEV
        range_index = (jnp.arange(CODES) // MP).astype(jnp.int32)
        is_live = pair_list < NA * NP
        a_pick = range_index[None, :] * NA + jnp.minimum(pair_list // NP, NA - 1)
        p_pick = range_index[None, :] * NP + pair_list % NP
        a_sel = a_row[a_pick] * is_live[:, :, None, None].astype(jnp.float32)
        p_sel = p_blocks[global_col[:, None], p_pick]
        return jnp.einsum("smij,smjk->sik", a_sel, p_sel, precision=lax.Precision.HIGHEST)

    return lax.map(one_row, (a_blocks, out_columns, pair_codes))
```

```python
import jax
import jax.numpy as jnp
from jax import lax
from jax.experimental import pallas as pl
from jax.experimental.pallas import tpu as pltpu
from jax.sharding import PartitionSpec as P

MESH = pl.DeviceIdType.MESH
BS = 128
SLOTS = 4
DEPTH = SLOTS * BS
MP = 7
NX, NY, NZ = 4, 8, 8
R1 = 224
GROUP = {1: (0, R1), 2: (R1, DEPTH - R1)}
RATE = 100e3
LAG = 1.5
FAR, NEAR = 5, 2


def onward(g, a, b):
    out = []
    if g == 1:
        if b == 0:
            if a == 0:
                out += [(1, 0, "x", 1), (-1, 0, "x", -1)]
            if a == 1:
                out += [(2, 0, "x", 1)]
            out += [(a, 1, "y", 1), (a, -1, "y", -1)]
        elif 0 < b < 4:
            out += [(a, b + 1, "y", 1)]
        elif -3 < b < 0:
            out += [(a, b - 1, "y", -1)]
    else:
        if a == 0:
            if b == 0:
                out += [(0, 1, "y", 1), (0, -1, "y", -1)]
            elif 0 < b < 4:
                out += [(0, b + 1, "y", 1)]
            elif -3 < b < 0:
                out += [(0, b - 1, "y", -1)]
            out += [(1, b, "x", 1), (-1, b, "x", -1)]
        elif a == 1:
            out += [(2, b, "x", 1)]
    return out


def arrivals():
    free = {"x": 0.0, "y": 0.0}
    queue = []
    count = 0

    def push(at, g, a, b):
        nonlocal count
        for a2, b2, axis, _ in onward(g, a, b):
            count += 1
            queue.append((at, count, g, a2, b2, axis))

    push(0.0, 2, 0, 0)
    push(0.0, 1, 0, 0)
    order = []
    while queue:
        queue.sort()
        at, _, g, a, b, axis = queue.pop(0)
        free[axis] = max(at, free[axis]) + GROUP[g][1] * BS * 4 / RATE
        order.append((free[axis] + LAG, (g, a, b)))
        push(free[axis] + LAG + 0.1, g, a, b)
    return sorted(order)


def kernel(
    a_ref, p_ref, cols_ref, codes_ref, out_ref,
    p_own, p_opp, ps_own, ps_opp, a_own, a_opp, b_own, b_opp, codes_own, codes_opp,
    p_recv, p_send, a_recv, a_send, sib_recv, sib_send, swap_send, codes_sem, local_sem,
):
    row, col, layer = lax.axis_index("row"), lax.axis_index("col"), lax.axis_index("layer")
    y, z, core = lax.rem(row, NY), col // 2, lax.rem(col, 2)
    x = (row // NY) * 2 + layer
    turn = 1 - 2 * core
    t = lax.rem(z + 2 * NZ - 4 * layer, NZ)
    q_me = row
    s_me = lax.rem(t, 4)

    def device(x_, y_, z_, core_):
        return ((x_ // 2) * NY + y_, z_ * 2 + core_, lax.rem(x_, 2))

    def along(axis, way):
        if axis == "x":
            return device(lax.rem(x + NX + turn * way, NX), y, z, core)
        if axis == "y":
            return device(x, lax.rem(y + NY + turn * way, NY), z, core)
        return device(x, y, lax.rem(z + NZ + way, NZ), core)

    sibling = device(x, y, z, 1 - core)
    partner = (row, col, 1 - layer)

    barrier = pltpu.get_barrier_semaphore()
    greeted = [along(axis, way) for axis in "xyz" for way in (1, -1)] + [sibling]
    for other in greeted:
        pl.semaphore_signal(barrier, inc=1, device_id=other, device_id_type=MESH)
    pl.semaphore_wait(barrier, len(greeted))

    p_land = (p_own, p_opp)
    p_split = (ps_own, ps_opp)
    a_land = (a_own, a_opp)
    b_parts = (b_own, b_opp)
    codes_land = (codes_own, codes_opp)

    def p_slot(a, b):
        x0 = lax.rem(x + 2 * NX - turn * a, NX)
        y0 = lax.rem(y + 2 * NY - turn * b, NY)
        return (x0 // 2) * NY + y0


    def p_piece(g, a, b):
        lo, size = GROUP[g]
        return p_land[a % 2].at[p_slot(a, b), pl.ds(lo, size)]

    def p_forward(g, a, b):
        lo, size = GROUP[g]
        src = p_ref.at[pl.ds(lo, size)] if (a, b) == (0, 0) else p_piece(g, a, b)
        copies = []
        for a2, b2, axis, way in onward(g, a, b):
            copies.append(
                pltpu.make_async_remote_copy(
                    src_ref=src,
                    dst_ref=p_land[a2 % 2].at[p_slot(a, b), pl.ds(lo, size)],
                    send_sem=p_send.at[g - 1, a2 + 1, b2 + 3],
                    recv_sem=p_recv.at[g - 1, a2 + 1, b2 + 3],
                    device_id=along(axis, way),
                    device_id_type=MESH,
                )
            )
        return copies

    def p_wait(g, a, b):
        here = p_piece(g, a, b)
        pltpu.make_async_remote_copy(
            src_ref=here,
            dst_ref=here,
            send_sem=p_send.at[g - 1, a + 1, b + 3],
            recv_sem=p_recv.at[g - 1, a + 1, b + 3],
            device_id=along("x", 1),
            device_id_type=MESH,
        ).wait_recv()

    def p_convert(a, b, lo, size):
        q = p_slot(a, b)
        value = p_land[a % 2][q, pl.ds(lo, size), :]
        high = value.astype(jnp.bfloat16)
        low = (value - high.astype(jnp.float32)).astype(jnp.bfloat16)
        p_split[a % 2][q, pl.ds(lo, size), pl.ds(0, BS)] = high
        p_split[a % 2][q, pl.ds(lo, size), pl.ds(BS, BS)] = low

    half = DEPTH // 2

    def a_rows(which, s, h):
        return a_land[which].at[2 * s + core, pl.ds(h * half, half)]

    def a_copy(which, h, s, d, way, src):
        return pltpu.make_async_remote_copy(
            src_ref=src,
            dst_ref=a_rows(which, s, h),
            send_sem=a_send.at[which, h, (1 - way) // 2, d],
            recv_sem=a_recv.at[which, h, s],
            device_id=along("z", way),
            device_id_type=MESH,
        )

    def a_wait(which, h, s):
        here = a_rows(which, s, h)
        pltpu.make_async_remote_copy(
            src_ref=here,
            dst_ref=here,
            send_sem=a_send.at[which, h, 0, 0],
            recv_sem=a_recv.at[which, h, s],
            device_id=along("z", 1),
            device_id_type=MESH,
        ).wait_recv()

    def sib_copy(which, s, src=None):
        here = a_land[which].at[2 * s + core]
        return pltpu.make_async_remote_copy(
            src_ref=here if src is None else src,
            dst_ref=here,
            send_sem=sib_send.at[which, s],
            recv_sem=sib_recv.at[which, s],
            device_id=sibling,
            device_id_type=MESH,
        )

    def sib_wait(which, s):
        there = a_land[which].at[2 * s + 1 - core]
        pltpu.make_async_remote_copy(
            src_ref=there,
            dst_ref=there,
            send_sem=sib_send.at[which, s],
            recv_sem=sib_recv.at[which, s],
            device_id=sibling,
            device_id_type=MESH,
        ).wait_recv()

    def swap_copy(h):
        return pltpu.make_async_remote_copy(
            src_ref=a_ref.at[pl.ds(h * half, half)],
            dst_ref=a_opp.at[2 * s_me + core, pl.ds(h * half, half)],
            send_sem=swap_send.at[h],
            recv_sem=a_recv.at[1, h, s_me],
            device_id=partner,
            device_id_type=MESH,
        )

    def moving(d, way):
        s = lax.rem(t + 2 * NZ - way * d, NZ)
        far = jnp.logical_and(s >= 2, s < 4) if way == 1 else s < 2
        valid = far if d > NEAR else s < 4
        goes_on = jnp.logical_and(valid, far) if d >= NEAR else valid
        if d == FAR:
            goes_on = None
        return lax.rem(s, 4), valid, goes_on

    codes_own[...] = jnp.full(codes_own.shape, SLOTS * SLOTS, jnp.int32)
    codes_own[:, pl.ds(0, SLOTS), pl.ds(0, MP)] = codes_ref[...]
    codes_copy = pltpu.make_async_remote_copy(
        src_ref=codes_own.at[pl.ds(8 * (1 - layer), 8)],
        dst_ref=codes_opp,
        send_sem=codes_sem.at[0],
        recv_sem=codes_sem.at[1],
        device_id=partner,
        device_id_type=MESH,
    )

    def combine(which, s):
        def step(i, carry):
            r, o = 2 * s + i // SLOTS, lax.rem(i, SLOTS)
            code_row = 8 * layer + r if which == 0 else r
            codes = codes_land[which][code_row, pl.ds(o, 1), :]
            index = lax.broadcasted_iota(jnp.int32, (SLOTS * SLOTS, BS), 0)
            live = jnp.zeros((SLOTS * SLOTS, BS), jnp.float32)
            for m in range(MP):
                live += (codes[:, m : m + 1] == index).astype(jnp.float32)
            strip = 32
            for k in range(BS // strip):
                parts = [a_land[which][r, pl.ds(a * BS + k * strip, strip), :] for a in range(SLOTS)]
                for p in range(SLOTS):
                    total = parts[0] * live[p : p + 1]
                    for a in range(1, SLOTS):
                        total += parts[a] * live[a * SLOTS + p : a * SLOTS + p + 1]
                    high = total.astype(jnp.bfloat16)
                    low = (total - high.astype(jnp.float32)).astype(jnp.bfloat16)
                    b_parts[which][r * SLOTS + o, pl.ds(k * strip, strip), pl.ds(p * BS, BS)] = high
                    b_parts[which][r * SLOTS + o, pl.ds(BS + k * strip, strip), pl.ds(p * BS, BS)] = low
            return carry

        lax.fori_loop(0, 2 * SLOTS, step, 0)

    def products(which):
        unroll = 4

        def step(i, carry):
            for j in range(unroll):
                o = i * unroll + j
                q = cols_ref[8 * layer + o // SLOTS, lax.rem(o, SLOTS)]
                four = jnp.dot(b_parts[which][o], p_split[which][q], preferred_element_type=jnp.float32)
                value = (four[BS:, BS:] + four[:BS, BS:] + four[BS:, :BS]) + four[:BS, :BS]
                out_ref[o] = value if which == 1 else out_ref[o] + value
            return carry

        lax.fori_loop(0, 8 * SLOTS // unroll, step, 0)

    events = []
    started = []

    def add(at, act):
        events.append((at, len(events), act))

    p_local = pltpu.make_async_copy(p_ref, p_own.at[q_me], local_sem.at[0])
    a_local = pltpu.make_async_copy(a_ref, a_own.at[2 * s_me + core], local_sem.at[1])

    def start():
        for copy in p_forward(2, 0, 0) + p_forward(1, 0, 0):
            copy.start()

        @pl.when(t < 4)
        def _():
            for h in range(2):
                for way in (1, -1):
                    a_copy(0, h, s_me, 0, way, a_ref.at[pl.ds(h * half, half)]).start()
            a_local.start()
            sib_copy(0, s_me, a_ref).start()

        @pl.when(t >= 4)
        def _():
            for h in range(2):
                swap_copy(h).start()

        codes_copy.start()
        p_local.start()

    def own_convert():
        p_local.wait()
        p_convert(0, 0, 0, DEPTH)

    def codes_arrive():
        codes_copy.wait()

    add(0.0, start)
    add(2.0, own_convert)
    add(2.5, codes_arrive)

    def p_event(g, a, b):
        def act():
            p_wait(g, a, b)
            for copy in p_forward(g, a, b):
                copy.start()
            p_convert(a, b, *GROUP[g])

        return act

    planned = arrivals()
    for at, (g, a, b) in planned:
        add(at, p_event(g, a, b))
    opp_done = max(at for at, (g, a, b) in planned if a % 2)
    last_sent = max(at for at, (g, a, b) in planned if onward(g, a, b))
    last = max(at for at, _ in planned)

    def self_event(which, h):
        def act():
            @pl.when(t < 4)
            def _():
                a_wait(1, h, s_me)
                for way in (1, -1):
                    a_copy(1, h, s_me, 0, way, a_rows(1, s_me, h)).start()
                if h == 1:
                    sib_copy(1, s_me).start()

        return act

    def self_combine(which):
        def act():
            @pl.when(t < 4)
            def _():
                if which == 0:
                    a_local.wait()
                sib_wait(which, s_me)
                combine(which, s_me)

        return act

    def hop_event(which, h, d, way):
        def act():
            s, valid, goes_on = moving(d, way)

            @pl.when(valid)
            def _():
                a_wait(which, h, s)
                if goes_on is not None:

                    @pl.when(goes_on)
                    def _():
                        a_copy(which, h, s, d, way, a_rows(which, s, h)).start()

                if h == 1:
                    sib_copy(which, s).start()

        return act

    def hop_combine(which, d, way):
        def act():
            s, valid, _ = moving(d, way)

            @pl.when(valid)
            def _():
                sib_wait(which, s)
                combine(which, s)

        return act

    for h in range(2):
        add(7.0 + 2.6 * h, self_event(1, h))
    add(5.0, self_combine(0))
    add(14.0, self_combine(1))
    for which in range(2):
        for d in range(1, FAR + 1):
            for h in range(2):
                at = 4.0 + 4.2 * d + 2.6 * h + 10.0 * which
                for way in (1, -1):
                    add(at, hop_event(which, h, d, way))
            for way in (1, -1):
                add(at + 3.0, hop_combine(which, d, way))
    b_opp_done = at + 3.0

    add(max(max(opp_done, last_sent), b_opp_done) + 0.05, lambda: products(1))
    add(max(last, b_opp_done) + 0.1, lambda: products(0))

    for _, _, act in sorted(events, key=lambda e: e[:2]):
        act()

    for g in (1, 2):
        for a in range(-1, 3):
            for b in range(-3, 5):
                for copy in p_forward(g, a, b):
                    copy.wait_send()

    @pl.when(t < 4)
    def _():
        for which in range(2):
            for h in range(2):
                for way in (1, -1):
                    a_copy(which, h, s_me, 0, way, a_rows(which, s_me, h)).wait_send()
            sib_copy(which, s_me).wait_send()

    @pl.when(t >= 4)
    def _():
        for h in range(2):
            swap_copy(h).wait_send()

    for which in range(2):
        for d in range(1, FAR + 1):
            for way in (1, -1):
                s, valid, goes_on = moving(d, way)

                @pl.when(valid)
                def _():
                    sib_copy(which, s).wait_send()

                if goes_on is not None:

                    @pl.when(goes_on)
                    def _():
                        for h in range(2):
                            a_copy(which, h, s, d, way, a_rows(which, s, h)).wait_send()


def shards(a_blocks, p_blocks, out_columns, pair_codes):
    vmem, smem, anywhere = pltpu.VMEM, pltpu.SMEM, pl.ANY
    dma = pltpu.SemaphoreType.DMA
    f32, bf16 = jnp.float32, jnp.bfloat16
    product = pl.pallas_call(
        kernel,
        out_shape=jax.ShapeDtypeStruct((8 * SLOTS, BS, BS), f32),
        in_specs=[
            pl.BlockSpec(memory_space=anywhere),
            pl.BlockSpec(memory_space=anywhere),
            pl.BlockSpec(memory_space=smem),
            pl.BlockSpec(memory_space=vmem),
        ],
        out_specs=pl.BlockSpec(memory_space=vmem),
        scratch_shapes=[
            vmem((16, DEPTH, BS), f32),
            vmem((16, DEPTH, BS), f32),
            vmem((16, DEPTH, 2 * BS), bf16),
            vmem((16, DEPTH, 2 * BS), bf16),
            vmem((8, DEPTH, BS), f32),
            vmem((8, DEPTH, BS), f32),
            vmem((8 * SLOTS, 2 * BS, DEPTH), bf16),
            vmem((8 * SLOTS, 2 * BS, DEPTH), bf16),
            vmem((16, 8, BS), jnp.int32),
            vmem((8, 8, BS), jnp.int32),
            dma((2, 4, 8)),
            dma((2, 4, 8)),
            dma((2, 2, 4)),
            dma((2, 2, 2, FAR + 1)),
            dma((2, 4)),
            dma((2, 4)),
            dma((2,)),
            dma((2,)),
            dma((2,)),
        ],
        compiler_params=pltpu.CompilerParams(
            collective_id=0, has_side_effects=True, vmem_limit_bytes=56 * 2**20
        ),
        cost_estimate=pl.CostEstimate(flops=4 * 10**9, bytes_accessed=5 * 2**20, transcendentals=0),
    )(
        a_blocks.reshape(DEPTH, BS),
        p_blocks.reshape(DEPTH, BS),
        out_columns,
        pair_codes,
    )
    return product.reshape(8, SLOTS, BS, BS)


def solution(mesh):
    return jax.shard_map(
        shards,
        mesh=mesh,
        in_specs=(
            P(("row", "col"), "layer", None, None),
            P(("row", "col"), "layer", None, None),
            P("row", "col"),
            P("row", "col", "layer"),
        ),
        out_specs=P(("row", "layer"), "col", None, None),
        check_vma=False,
    )
```

```python
import jax
import jax.numpy as jnp
from jax import lax
from jax.experimental import pallas as pl
from jax.experimental.pallas import tpu as pltpu
from jax.sharding import PartitionSpec as P

MESH = pl.DeviceIdType.MESH
BS = 128
SLOTS = 4
DEPTH = SLOTS * BS
MP = 7
NX, NY, NZ = 4, 8, 8
R1 = 224
GROUP = {1: (0, R1), 2: (R1, DEPTH - R1)}
RATE = 100e3
LAG = 1.5
FAR, NEAR = 5, 2


def onward(g, a, b):
    out = []
    if g == 1:
        if b == 0:
            if a == 0:
                out += [(1, 0, "x", 1), (-1, 0, "x", -1)]
            if a == 1:
                out += [(2, 0, "x", 1)]
            out += [(a, 1, "y", 1), (a, -1, "y", -1)]
        elif 0 < b < 4:
            out += [(a, b + 1, "y", 1)]
        elif -3 < b < 0:
            out += [(a, b - 1, "y", -1)]
    else:
        if a == 0:
            if b == 0:
                out += [(0, 1, "y", 1), (0, -1, "y", -1)]
            elif 0 < b < 4:
                out += [(0, b + 1, "y", 1)]
            elif -3 < b < 0:
                out += [(0, b - 1, "y", -1)]
            out += [(1, b, "x", 1), (-1, b, "x", -1)]
        elif a == 1:
            out += [(2, b, "x", 1)]
    return out


def arrivals():
    free = {"x": 0.0, "y": 0.0}
    queue = []
    count = 0

    def push(at, g, a, b):
        nonlocal count
        for a2, b2, axis, _ in onward(g, a, b):
            count += 1
            queue.append((at, count, g, a2, b2, axis))

    push(0.0, 2, 0, 0)
    push(0.0, 1, 0, 0)
    order = []
    while queue:
        queue.sort()
        at, _, g, a, b, axis = queue.pop(0)
        free[axis] = max(at, free[axis]) + GROUP[g][1] * BS * 4 / RATE
        order.append((free[axis] + LAG, (g, a, b)))
        push(free[axis] + LAG + 0.1, g, a, b)
    return sorted(order)


def kernel(
    a_ref, p_ref, cols_ref, codes_ref, out_ref,
    p_own, p_opp, ps_own, ps_opp, a_own, a_opp, sums_own, sums_opp, codes_own, codes_opp,
    picks_own, picks_opp, picks_smem_own, picks_smem_opp,
    p_recv, p_send, a_recv, a_send, sib_recv, sib_send, swap_send, codes_sem, local_sem,
):
    row, col, layer = lax.axis_index("row"), lax.axis_index("col"), lax.axis_index("layer")
    y, z, core = lax.rem(row, NY), col // 2, lax.rem(col, 2)
    x = (row // NY) * 2 + layer
    turn = 1 - 2 * core
    t = lax.rem(z + 2 * NZ - 4 * layer, NZ)
    q_me = row
    s_me = lax.rem(t, 4)

    def device(x_, y_, z_, core_):
        return ((x_ // 2) * NY + y_, z_ * 2 + core_, lax.rem(x_, 2))

    def along(axis, way):
        if axis == "x":
            return device(lax.rem(x + NX + turn * way, NX), y, z, core)
        if axis == "y":
            return device(x, lax.rem(y + NY + turn * way, NY), z, core)
        return device(x, y, lax.rem(z + NZ + way, NZ), core)

    sibling = device(x, y, z, 1 - core)
    partner = (row, col, 1 - layer)

    barrier = pltpu.get_barrier_semaphore()
    greeted = [along(axis, way) for axis in "xyz" for way in (1, -1)] + [sibling]
    for other in greeted:
        pl.semaphore_signal(barrier, inc=1, device_id=other, device_id_type=MESH)
    pl.semaphore_wait(barrier, len(greeted))

    p_land = (p_own, p_opp)
    p_split = (ps_own, ps_opp)
    a_land = (a_own, a_opp)
    sums = (sums_own, sums_opp)
    picks = (picks_own, picks_opp)
    picks_smem = (picks_smem_own, picks_smem_opp)
    codes_land = (codes_own, codes_opp)

    def p_slot(a, b):
        x0 = lax.rem(x + 2 * NX - turn * a, NX)
        y0 = lax.rem(y + 2 * NY - turn * b, NY)
        return (x0 // 2) * NY + y0


    def p_piece(g, a, b):
        lo, size = GROUP[g]
        return p_land[a % 2].at[p_slot(a, b), pl.ds(lo, size)]

    def p_forward(g, a, b):
        lo, size = GROUP[g]
        src = p_ref.at[pl.ds(lo, size)] if (a, b) == (0, 0) else p_piece(g, a, b)
        copies = []
        for a2, b2, axis, way in onward(g, a, b):
            copies.append(
                pltpu.make_async_remote_copy(
                    src_ref=src,
                    dst_ref=p_land[a2 % 2].at[p_slot(a, b), pl.ds(lo, size)],
                    send_sem=p_send.at[g - 1, a2 + 1, b2 + 3],
                    recv_sem=p_recv.at[g - 1, a2 + 1, b2 + 3],
                    device_id=along(axis, way),
                    device_id_type=MESH,
                )
            )
        return copies

    def p_wait(g, a, b):
        here = p_piece(g, a, b)
        pltpu.make_async_remote_copy(
            src_ref=here,
            dst_ref=here,
            send_sem=p_send.at[g - 1, a + 1, b + 3],
            recv_sem=p_recv.at[g - 1, a + 1, b + 3],
            device_id=along("x", 1),
            device_id_type=MESH,
        ).wait_recv()

    def p_convert(a, b, lo, size):
        q = p_slot(a, b)
        value = p_land[a % 2][q, pl.ds(lo, size), :]
        high = value.astype(jnp.bfloat16)
        low = (value - high.astype(jnp.float32)).astype(jnp.bfloat16)
        p_split[a % 2][q, pl.ds(lo, size), pl.ds(0, BS)] = high
        p_split[a % 2][q, pl.ds(lo, size), pl.ds(BS, BS)] = low

    half = DEPTH // 2

    def a_rows(which, s, h):
        return a_land[which].at[2 * s + core, pl.ds(h * half, half)]

    def a_copy(which, h, s, d, way, src):
        return pltpu.make_async_remote_copy(
            src_ref=src,
            dst_ref=a_rows(which, s, h),
            send_sem=a_send.at[which, h, (1 - way) // 2, d],
            recv_sem=a_recv.at[which, h, s],
            device_id=along("z", way),
            device_id_type=MESH,
        )

    def a_wait(which, h, s):
        here = a_rows(which, s, h)
        pltpu.make_async_remote_copy(
            src_ref=here,
            dst_ref=here,
            send_sem=a_send.at[which, h, 0, 0],
            recv_sem=a_recv.at[which, h, s],
            device_id=along("z", 1),
            device_id_type=MESH,
        ).wait_recv()

    def sib_copy(which, s, src=None):
        here = a_land[which].at[2 * s + core]
        return pltpu.make_async_remote_copy(
            src_ref=here if src is None else src,
            dst_ref=here,
            send_sem=sib_send.at[which, s],
            recv_sem=sib_recv.at[which, s],
            device_id=sibling,
            device_id_type=MESH,
        )

    def sib_wait(which, s):
        there = a_land[which].at[2 * s + 1 - core]
        pltpu.make_async_remote_copy(
            src_ref=there,
            dst_ref=there,
            send_sem=sib_send.at[which, s],
            recv_sem=sib_recv.at[which, s],
            device_id=sibling,
            device_id_type=MESH,
        ).wait_recv()

    def swap_copy(h):
        return pltpu.make_async_remote_copy(
            src_ref=a_ref.at[pl.ds(h * half, half)],
            dst_ref=a_opp.at[2 * s_me + core, pl.ds(h * half, half)],
            send_sem=swap_send.at[h],
            recv_sem=a_recv.at[1, h, s_me],
            device_id=partner,
            device_id_type=MESH,
        )

    def moving(d, way):
        s = lax.rem(t + 2 * NZ - way * d, NZ)
        far = jnp.logical_and(s >= 2, s < 4) if way == 1 else s < 2
        valid = far if d > NEAR else s < 4
        goes_on = jnp.logical_and(valid, far) if d >= NEAR else valid
        if d == FAR:
            goes_on = None
        return lax.rem(s, 4), valid, goes_on

    codes_own[...] = jnp.full(codes_own.shape, SLOTS * SLOTS, jnp.int32)
    codes_own[:, pl.ds(0, SLOTS), pl.ds(0, 16)] = codes_ref[...]
    codes_copy = pltpu.make_async_remote_copy(
        src_ref=codes_own,
        dst_ref=codes_opp,
        send_sem=codes_sem.at[0],
        recv_sem=codes_sem.at[1],
        device_id=partner,
        device_id_type=MESH,
    )

    def pick_copy(which):
        return pltpu.make_async_copy(picks[which], picks_smem[which], local_sem.at[2 + which])

    def pick(which):
        codes = [codes_land[which][m] for m in range(MP)]
        for p in range(SLOTS):
            total = jnp.zeros((8, BS), jnp.int32)
            for code in codes:
                for a in range(SLOTS):
                    total += jnp.where(code == a * SLOTS + p, 1 << a, 0)
            picks[which][p] = total
        pick_copy(which).start()

    def combine(which, s):
        def step(i, carry):
            r = 2 * s + i
            strip = 16
            for k in range(BS // strip):
                total = {0: None}
                for n in range(1, 16):
                    a = n.bit_length() - 1
                    part = a_land[which][r, pl.ds(a * BS + k * strip, strip), :] if n == 1 << a else None
                    total[n] = part if n == 1 << a else total[n - (1 << a)] + total[1 << a]
                    high = total[n].astype(jnp.bfloat16)
                    low = (total[n] - high.astype(jnp.float32)).astype(jnp.bfloat16)
                    sums[which][r, n, pl.ds(k * strip, strip), :] = high
                    sums[which][r, n, pl.ds(BS + k * strip, strip), :] = low
            return carry

        lax.fori_loop(0, 2, step, 0)

    def products(which):
        pick_copy(which).wait()

        def step(r, carry):
            at = 8 * layer + r
            for o in range(SLOTS):
                q = cols_ref[o, at]
                left = jnp.concatenate([sums[which][r, picks_smem[which][p, o, at]] for p in range(SLOTS)], axis=1)
                four = jnp.dot(left, p_split[which][q], preferred_element_type=jnp.float32)
                value = (four[BS:, BS:] + four[:BS, BS:] + four[BS:, :BS]) + four[:BS, :BS]
                where = r * SLOTS + o
                out_ref[where] = value if which == 1 else out_ref[where] + value
            return carry

        lax.fori_loop(0, 8, step, 0)

    events = []
    started = []

    def add(at, act):
        events.append((at, len(events), act))

    p_local = pltpu.make_async_copy(p_ref, p_own.at[q_me], local_sem.at[0])
    a_local = pltpu.make_async_copy(a_ref, a_own.at[2 * s_me + core], local_sem.at[1])

    def start():
        for copy in p_forward(2, 0, 0) + p_forward(1, 0, 0):
            copy.start()

        @pl.when(t < 4)
        def _():
            for h in range(2):
                for way in (1, -1):
                    a_copy(0, h, s_me, 0, way, a_ref.at[pl.ds(h * half, half)]).start()
            a_local.start()
            sib_copy(0, s_me, a_ref).start()

        @pl.when(t >= 4)
        def _():
            for h in range(2):
                swap_copy(h).start()

        codes_copy.start()
        p_local.start()
        for which in range(2):
            sums[which][:, 0] = jnp.zeros((8, 2 * BS, BS), jnp.bfloat16)
        pick(0)

    def own_convert():
        p_local.wait()
        p_convert(0, 0, 0, DEPTH)

    def codes_arrive():
        codes_copy.wait()
        pick(1)

    add(0.0, start)
    add(2.0, own_convert)
    add(2.5, codes_arrive)

    def p_event(g, a, b):
        def act():
            p_wait(g, a, b)
            for copy in p_forward(g, a, b):
                copy.start()
            p_convert(a, b, *GROUP[g])

        return act

    planned = arrivals()
    for at, (g, a, b) in planned:
        add(at, p_event(g, a, b))
    opp_done = max(at for at, (g, a, b) in planned if a % 2)
    last_sent = max(at for at, (g, a, b) in planned if onward(g, a, b))
    last = max(at for at, _ in planned)

    def self_event(which, h):
        def act():
            @pl.when(t < 4)
            def _():
                a_wait(1, h, s_me)
                for way in (1, -1):
                    a_copy(1, h, s_me, 0, way, a_rows(1, s_me, h)).start()
                if h == 1:
                    sib_copy(1, s_me).start()

        return act

    def self_combine(which):
        def act():
            @pl.when(t < 4)
            def _():
                if which == 0:
                    a_local.wait()
                sib_wait(which, s_me)
                combine(which, s_me)

        return act

    def hop_event(which, h, d, way):
        def act():
            s, valid, goes_on = moving(d, way)

            @pl.when(valid)
            def _():
                a_wait(which, h, s)
                if goes_on is not None:

                    @pl.when(goes_on)
                    def _():
                        a_copy(which, h, s, d, way, a_rows(which, s, h)).start()

                if h == 1:
                    sib_copy(which, s).start()

        return act

    def hop_combine(which, d, way):
        def act():
            s, valid, _ = moving(d, way)

            @pl.when(valid)
            def _():
                sib_wait(which, s)
                combine(which, s)

        return act

    for h in range(2):
        add(7.0 + 2.6 * h, self_event(1, h))
    add(5.0, self_combine(0))
    add(14.0, self_combine(1))
    for which in range(2):
        for d in range(1, FAR + 1):
            for h in range(2):
                at = 4.0 + 4.2 * d + 2.6 * h + 10.0 * which
                for way in (1, -1):
                    add(at, hop_event(which, h, d, way))
            for way in (1, -1):
                add(at + 3.0, hop_combine(which, d, way))
    b_opp_done = at + 3.0

    add(max(max(opp_done, last_sent), b_opp_done) + 0.05, lambda: products(1))
    add(max(last, b_opp_done) + 0.1, lambda: products(0))

    for _, _, act in sorted(events, key=lambda e: e[:2]):
        act()

    for g in (1, 2):
        for a in range(-1, 3):
            for b in range(-3, 5):
                for copy in p_forward(g, a, b):
                    copy.wait_send()

    @pl.when(t < 4)
    def _():
        for which in range(2):
            for h in range(2):
                for way in (1, -1):
                    a_copy(which, h, s_me, 0, way, a_rows(which, s_me, h)).wait_send()
            sib_copy(which, s_me).wait_send()

    @pl.when(t >= 4)
    def _():
        for h in range(2):
            swap_copy(h).wait_send()

    for which in range(2):
        for d in range(1, FAR + 1):
            for way in (1, -1):
                s, valid, goes_on = moving(d, way)

                @pl.when(valid)
                def _():
                    sib_copy(which, s).wait_send()

                if goes_on is not None:

                    @pl.when(goes_on)
                    def _():
                        for h in range(2):
                            a_copy(which, h, s, d, way, a_rows(which, s, h)).wait_send()


def shards(a_blocks, p_blocks, out_columns, pair_codes):
    vmem, smem, anywhere = pltpu.VMEM, pltpu.SMEM, pl.ANY
    dma = pltpu.SemaphoreType.DMA
    f32, bf16 = jnp.float32, jnp.bfloat16
    product = pl.pallas_call(
        kernel,
        out_shape=jax.ShapeDtypeStruct((8 * SLOTS, BS, BS), f32),
        in_specs=[
            pl.BlockSpec(memory_space=anywhere),
            pl.BlockSpec(memory_space=anywhere),
            pl.BlockSpec(memory_space=smem),
            pl.BlockSpec(memory_space=vmem),
        ],
        out_specs=pl.BlockSpec(memory_space=vmem),
        scratch_shapes=[
            vmem((16, DEPTH, BS), f32),
            vmem((16, DEPTH, BS), f32),
            vmem((16, DEPTH, 2 * BS), bf16),
            vmem((16, DEPTH, 2 * BS), bf16),
            vmem((8, DEPTH, BS), f32),
            vmem((8, DEPTH, BS), f32),
            vmem((8, 16, 2 * BS, BS), bf16),
            vmem((8, 16, 2 * BS, BS), bf16),
            vmem((MP, 8, BS), jnp.int32),
            vmem((MP, 8, BS), jnp.int32),
            vmem((SLOTS, 8, BS), jnp.int32),
            vmem((SLOTS, 8, BS), jnp.int32),
            smem((SLOTS, 8, BS), jnp.int32),
            smem((SLOTS, 8, BS), jnp.int32),
            dma((2, 4, 8)),
            dma((2, 4, 8)),
            dma((2, 2, 4)),
            dma((2, 2, 2, FAR + 1)),
            dma((2, 4)),
            dma((2, 4)),
            dma((2,)),
            dma((2,)),
            dma((4,)),
        ],
        compiler_params=pltpu.CompilerParams(
            collective_id=0, has_side_effects=True, vmem_limit_bytes=44 * 2**20
        ),
        cost_estimate=pl.CostEstimate(flops=4 * 10**9, bytes_accessed=5 * 2**20, transcendentals=0),
    )(
        a_blocks.reshape(DEPTH, BS),
        p_blocks.reshape(DEPTH, BS),
        out_columns.T,
        pair_codes.transpose(2, 1, 0),
    )
    return product.reshape(8, SLOTS, BS, BS)


def solution(mesh):
    return jax.shard_map(
        shards,
        mesh=mesh,
        in_specs=(
            P(("row", "col"), "layer", None, None),
            P(("row", "col"), "layer", None, None),
            P("row", "col"),
            P("row", "col", "layer"),
        ),
        out_specs=P(("row", "layer"), "col", None, None),
        check_vma=False,
    )
```

```python
import jax
import jax.numpy as jnp
from jax import lax
from jax.experimental import pallas as pl
from jax.experimental.pallas import tpu as pltpu
from jax.sharding import PartitionSpec as P

MESH = pl.DeviceIdType.MESH
BS = 128
SLOTS = 4
DEPTH = SLOTS * BS
MP = 7
NX, NY, NZ = 4, 8, 8
R1 = 224
GROUP = {1: (0, R1), 2: (R1, DEPTH - R1)}
ORDER = (
    ("P", 1, 0, -1), ("P", 1, 0, 1), ("P", 2, 0, -1), ("P", 1, -1, 0), ("P", 2, 0, 1), ("P", 1, 1, 0), ("P", 2, 1, 0),
    ("P", 2, -1, 0), ("P", 2, 0, 2), ("P", 2, 1, 1), ("P", 1, 0, 2), ("P", 2, -1, 1), ("P", 1, 1, 1), ("P", 2, 0, -2),
    ("P", 1, 0, -2), ("P", 2, -1, -1), ("P", 1, -1, -1), ("P", 1, -1, 1), ("P", 2, 2, 0), ("P", 1, 1, -1),
    ("P", 1, 2, 0), ("P", 2, 1, -1), ("M", 0), ("P", 2, -1, 2), ("P", 2, 0, 3), ("P", 2, 2, 1), ("P", 2, 1, 2),
    ("M", 1), ("H", 1, 1, 0), ("P", 1, 1, 2), ("H", 1, -1, 0), ("H", 1, -1, 1), ("P", 2, 1, -2), ("P", 2, -1, -2),
    ("H", 1, 1, 1), ("P", 1, 0, 3), ("C", 0, 1), ("P", 2, 2, -1), ("P", 2, 0, -3), ("P", 1, -1, 2), ("P", 1, 1, -2),
    ("P", 1, 2, 1), ("P", 1, -1, -2), ("P", 1, 2, -1), ("H", 2, 1, 0), ("C", 1, -1), ("P", 1, 0, -3), ("P", 2, 1, 3),
    ("C", 1, 1), ("P", 2, -1, 3), ("P", 2, 2, 2), ("H", 2, 1, 1), ("P", 2, 0, 4), ("H", 2, -1, 0), ("H", 2, -1, 1),
    ("H", 3, 1, 0), ("P", 1, 1, 3), ("C", 2, 1), ("C", 2, -1), ("H", 3, -1, 0), ("P", 2, -1, -3), ("P", 2, 1, -3),
    ("H", 3, 1, 1), ("P", 2, 2, -2), ("P", 1, 1, -3), ("P", 1, 0, 4), ("P", 1, -1, 3), ("H", 3, -1, 1),
    ("H", 4, 1, 0), ("P", 1, 2, 2), ("P", 1, 2, -2), ("C", 3, 1), ("P", 1, -1, -3), ("C", 3, -1), ("H", 4, 1, 1),
    ("P", 1, 1, 4), ("P", 2, 2, 3), ("P", 2, -1, 4), ("C", 4, 1), ("P", 2, 1, 4), ("P", 2, 2, -3), ("P", 1, -1, 4),
    ("P", 1, 2, 3), ("P", 2, 2, 4), ("P", 1, 2, -3), ("P", 1, 2, 4),
)


def onward(g, a, b):
    out = []
    if g == 1:
        if b == 0:
            if a == 0:
                out += [(1, 0, "x", 1), (-1, 0, "x", -1)]
            if a == 1:
                out += [(2, 0, "x", 1)]
            out += [(a, 1, "y", 1), (a, -1, "y", -1)]
        elif 0 < b < 4:
            out += [(a, b + 1, "y", 1)]
        elif -3 < b < 0:
            out += [(a, b - 1, "y", -1)]
    else:
        if a == 0:
            if b == 0:
                out += [(0, 1, "y", 1), (0, -1, "y", -1)]
            elif 0 < b < 4:
                out += [(0, b + 1, "y", 1)]
            elif -3 < b < 0:
                out += [(0, b - 1, "y", -1)]
            out += [(1, b, "x", 1), (-1, b, "x", -1)]
        elif a == 1:
            out += [(2, b, "x", 1)]
    return out


def kernel(
    a_ref, p_ref, cols_ref, codes_ref, out_ref,
    p_own, p_opp, ps_own, ps_opp, a_all, sums, cols, codes_in, codes_own, codes_opp,
    picks_own, picks_opp, picks_smem_own, picks_smem_opp,
    p_recv, p_send, a_recv, a_send, sib_recv, sib_send, move_send, codes_sem, local_sem,
):
    row, col, layer = lax.axis_index("row"), lax.axis_index("col"), lax.axis_index("layer")
    y, z, core = lax.rem(row, NY), col // 2, lax.rem(col, 2)
    x = (row // NY) * 2 + layer
    turn = 1 - 2 * core
    t = lax.rem(z + 2 * NZ - 4 * layer, NZ)
    q_me = row

    def device(x_, y_, z_, core_):
        return ((x_ // 2) * NY + y_, z_ * 2 + core_, lax.rem(x_, 2))

    def along(axis, way):
        if axis == "x":
            return device(lax.rem(x + NX + turn * way, NX), y, z, core)
        if axis == "y":
            return device(x, lax.rem(y + NY + turn * way, NY), z, core)
        return device(x, y, lax.rem(z + NZ + turn * way, NZ), core)

    sibling = device(x, y, z, 1 - core)
    partner = (row, col, 1 - layer)
    mover = (row, (NZ - 1 - z) * 2 + core, 1 - layer)

    codes_load = pltpu.make_async_copy(codes_ref, codes_in, local_sem.at[4])
    cols_load = pltpu.make_async_copy(cols_ref, cols, local_sem.at[5])
    codes_load.start()
    cols_load.start()

    barrier = pltpu.get_barrier_semaphore()
    greeted = [along(axis, way) for axis in "xyz" for way in (1, -1)] + [sibling, mover]
    for other in greeted:
        pl.semaphore_signal(barrier, inc=1, device_id=other, device_id_type=MESH)
    pl.semaphore_wait(barrier, len(greeted))

    p_land = (p_own, p_opp)
    p_split = (ps_own, ps_opp)
    picks = (picks_own, picks_opp)
    picks_smem = (picks_smem_own, picks_smem_opp)
    codes_land = (codes_own, codes_opp)

    def p_slot(a, b):
        x0 = lax.rem(x + 2 * NX - turn * a, NX)
        y0 = lax.rem(y + 2 * NY - turn * b, NY)
        return (x0 // 2) * NY + y0


    def p_piece(g, a, b):
        lo, size = GROUP[g]
        return p_land[a % 2].at[p_slot(a, b), pl.ds(lo, size)]

    def p_forward(g, a, b):
        lo, size = GROUP[g]
        src = p_ref.at[pl.ds(lo, size)] if (a, b) == (0, 0) else p_piece(g, a, b)
        copies = []
        for a2, b2, axis, way in onward(g, a, b):
            copies.append(
                pltpu.make_async_remote_copy(
                    src_ref=src,
                    dst_ref=p_land[a2 % 2].at[p_slot(a, b), pl.ds(lo, size)],
                    send_sem=p_send.at[g - 1, a2 + 1, b2 + 3],
                    recv_sem=p_recv.at[g - 1, a2 + 1, b2 + 3],
                    device_id=along(axis, way),
                    device_id_type=MESH,
                )
            )
        return copies

    def p_wait(g, a, b):
        here = p_piece(g, a, b)
        pltpu.make_async_remote_copy(
            src_ref=here,
            dst_ref=here,
            send_sem=p_send.at[g - 1, a + 1, b + 3],
            recv_sem=p_recv.at[g - 1, a + 1, b + 3],
            device_id=along("x", 1),
            device_id_type=MESH,
        ).wait_recv()

    def p_convert(a, b, lo, size):
        q = p_slot(a, b)
        value = p_land[a % 2][q, pl.ds(lo, size), :]
        high = value.astype(jnp.bfloat16)
        low = (value - high.astype(jnp.float32)).astype(jnp.bfloat16)
        p_split[a % 2][q, pl.ds(lo, size), pl.ds(0, BS)] = high
        p_split[a % 2][q, pl.ds(lo, size), pl.ds(BS, BS)] = low

    half = DEPTH // 2

    def rows_of(e):
        return jnp.where(e < 4, 2 * e, 8 + 2 * (7 - e))

    def a_half(e, h):
        return a_all.at[rows_of(e) + core, pl.ds(h * half, half)]

    def a_copy(e, h, d, way, src=None):
        return pltpu.make_async_remote_copy(
            src_ref=a_half(e, h) if src is None else src,
            dst_ref=a_half(e, h),
            send_sem=a_send.at[h, (1 - way) // 2, d],
            recv_sem=a_recv.at[h, e],
            device_id=along("z", way),
            device_id_type=MESH,
        )

    def a_wait(e, h):
        a_copy(e, h, 0, 1).wait_recv()

    def sib_copy(e, src=None):
        here = a_all.at[rows_of(e) + core]
        return pltpu.make_async_remote_copy(
            src_ref=here if src is None else src,
            dst_ref=here,
            send_sem=sib_send.at[e],
            recv_sem=sib_recv.at[e],
            device_id=sibling,
            device_id_type=MESH,
        )

    def sib_wait(e):
        there = a_all.at[rows_of(e) + 1 - core]
        pltpu.make_async_remote_copy(
            src_ref=there,
            dst_ref=there,
            send_sem=sib_send.at[e],
            recv_sem=sib_recv.at[e],
            device_id=sibling,
            device_id_type=MESH,
        ).wait_recv()

    def move_copy(h):
        return pltpu.make_async_remote_copy(
            src_ref=a_ref.at[pl.ds(h * half, half)],
            dst_ref=a_half(11 - t, h),
            send_sem=move_send.at[h],
            recv_sem=a_recv.at[h, 11 - t],
            device_id=mover,
            device_id_type=MESH,
        )

    def source(d, way):
        return lax.rem(t + 2 * NZ - turn * way * d, NZ)

    def goes_on(d, way):
        return d < (4 if way == 1 else 3)

    codes_copy = pltpu.make_async_remote_copy(
        src_ref=codes_own,
        dst_ref=codes_opp,
        send_sem=codes_sem.at[0],
        recv_sem=codes_sem.at[1],
        device_id=partner,
        device_id_type=MESH,
    )

    def pick_copy(which):
        return pltpu.make_async_copy(picks[which], picks_smem[which], local_sem.at[2 + which])

    def pick(which):
        codes = [codes_land[which][m] for m in range(MP)]
        for p in range(SLOTS):
            total = jnp.zeros((8, BS), jnp.int32)
            for code in codes:
                for a in range(SLOTS):
                    total += jnp.where(code == a * SLOTS + p, 1 << a, 0)
            picks[which][p] = total
        pick_copy(which).start()

    def combine(e):
        def step(i, carry):
            r = rows_of(e) + i
            strip = 16
            for k in range(BS // strip):
                total = {0: None}
                for n in range(1, 16):
                    a = n.bit_length() - 1
                    part = a_all[r, pl.ds(a * BS + k * strip, strip), :] if n == 1 << a else None
                    total[n] = part if n == 1 << a else total[n - (1 << a)] + total[1 << a]
                    high = total[n].astype(jnp.bfloat16)
                    low = (total[n] - high.astype(jnp.float32)).astype(jnp.bfloat16)
                    sums[r, n, pl.ds(k * strip, strip), :] = high
                    sums[r, n, pl.ds(BS + k * strip, strip), :] = low
            return carry

        lax.fori_loop(0, 2, step, 0)

    def products(which):
        pick_copy(which).wait()

        def step(r, carry):
            at = 8 * layer + r
            for o in range(SLOTS):
                q = cols[o, at]
                left = jnp.concatenate([sums[8 * which + r, picks_smem[which][p, o, at]] for p in range(SLOTS)], axis=1)
                four = jnp.dot(left, p_split[which][q], preferred_element_type=jnp.float32)
                value = (four[BS:, BS:] + four[:BS, BS:] + four[BS:, :BS]) + four[:BS, :BS]
                where = r * SLOTS + o
                out_ref[where] = value if which == 1 else out_ref[where] + value
            return carry

        lax.fori_loop(0, 8, step, 0)

    p_local = pltpu.make_async_copy(p_ref, p_own.at[q_me], local_sem.at[0])
    a_local = pltpu.make_async_copy(a_ref, a_all.at[rows_of(lax.rem(t, 4)) + core], local_sem.at[1])

    @pl.when(t >= 4)
    def _():
        for h in range(2):
            move_copy(h).start()

    for copy in p_forward(2, 0, 0) + p_forward(1, 0, 0):
        copy.start()

    @pl.when(t < 4)
    def _():
        for h in range(2):
            for way in (1, -1):
                a_copy(t, h, 0, way, a_ref.at[pl.ds(h * half, half)]).start()
        a_local.start()
        sib_copy(t, a_ref).start()

    p_local.start()
    codes_own[...] = jnp.full(codes_own.shape, SLOTS * SLOTS, jnp.int32)
    codes_load.wait()
    codes_own[:, pl.ds(0, SLOTS), pl.ds(0, 16)] = codes_in[...]
    codes_copy.start()
    cols_load.wait()
    pick(0)
    sums[:, 0] = jnp.zeros((16, 2 * BS, BS), jnp.bfloat16)
    p_local.wait()
    p_convert(0, 0, 0, DEPTH)
    codes_copy.wait()
    pick(1)

    def piece_of_p(g, a, b):
        p_wait(g, a, b)
        for copy in p_forward(g, a, b):
            copy.start()
        p_convert(a, b, *GROUP[g])

    def moved(h):
        @pl.when(t >= 4)
        def _():
            a_wait(t, h)
            for way in (1, -1):
                a_copy(t, h, 0, way).start()
            if h == 1:
                sib_copy(t).start()

    def hop(d, way, h):
        e = source(d, way)
        a_wait(e, h)
        if goes_on(d, way):
            a_copy(e, h, d, way).start()
        if h == 1:
            sib_copy(e).start()

    def add_up(d, way):
        if d == 0:

            @pl.when(t < 4)
            def _():
                a_local.wait()

        e = source(d, way)
        sib_wait(e)
        combine(e)

    steps = {"P": piece_of_p, "M": moved, "H": hop, "C": add_up}
    for name, *where in ORDER:
        steps[name](*where)
    products(1)
    products(0)

    for g in (1, 2):
        for a in range(-1, 3):
            for b in range(-3, 5):
                for copy in p_forward(g, a, b):
                    copy.wait_send()

    @pl.when(t >= 4)
    def _():
        for h in range(2):
            move_copy(h).wait_send()

    for d in range(5):
        for way in (1, -1):
            if (d == 4 and way == -1) or (d == 0 and way == -1):
                continue
            e = source(d, way)
            sib_copy(e).wait_send()
    for d in range(4):
        for way in (1, -1):
            if goes_on(d, way):
                for h in range(2):
                    a_copy(source(d, way), h, d, way).wait_send()


def shards(a_blocks, p_blocks, out_columns, pair_codes):
    vmem, smem = pltpu.VMEM, pltpu.SMEM
    dma = pltpu.SemaphoreType.DMA
    f32, bf16 = jnp.float32, jnp.bfloat16
    operands = (
        a_blocks.reshape(DEPTH, BS),
        p_blocks.reshape(DEPTH, BS),
        out_columns.T,
        pair_codes.transpose(2, 1, 0),
    )
    product = pl.pallas_call(
        kernel,
        out_shape=jax.ShapeDtypeStruct((8 * SLOTS, BS, BS), f32),
        in_specs=[
            pl.BlockSpec(memory_space=pltpu.HBM),
            pl.BlockSpec(memory_space=pltpu.HBM),
            pl.BlockSpec(memory_space=pltpu.HBM),
            pl.BlockSpec(memory_space=pltpu.HBM),
        ],
        out_specs=pl.BlockSpec(memory_space=vmem),
        scratch_shapes=[
            vmem((16, DEPTH, BS), f32),
            vmem((16, DEPTH, BS), f32),
            vmem((16, DEPTH, 2 * BS), bf16),
            vmem((16, DEPTH, 2 * BS), bf16),
            vmem((16, DEPTH, BS), f32),
            vmem((16, 16, 2 * BS, BS), bf16),
            smem((SLOTS, 16), jnp.int32),
            vmem((MP, SLOTS, 16), jnp.int32),
            vmem((MP, 8, BS), jnp.int32),
            vmem((MP, 8, BS), jnp.int32),
            vmem((SLOTS, 8, BS), jnp.int32),
            vmem((SLOTS, 8, BS), jnp.int32),
            smem((SLOTS, 8, BS), jnp.int32),
            smem((SLOTS, 8, BS), jnp.int32),
            dma((2, 4, 8)),
            dma((2, 4, 8)),
            dma((2, 8)),
            dma((2, 2, 4)),
            dma((8,)),
            dma((8,)),
            dma((2,)),
            dma((2,)),
            dma((6,)),
        ],
        compiler_params=pltpu.CompilerParams(
            collective_id=0, has_side_effects=True, vmem_limit_bytes=44 * 2**20
        ),
        cost_estimate=pl.CostEstimate(flops=4 * 10**9, bytes_accessed=5 * 2**20, transcendentals=0),
    )(*(pltpu.with_memory_space_constraint(operand, pltpu.HBM) for operand in operands))
    return product.reshape(8, SLOTS, BS, BS)


def solution(mesh):
    return jax.shard_map(
        shards,
        mesh=mesh,
        in_specs=(
            P(("row", "col"), "layer", None, None),
            P(("row", "col"), "layer", None, None),
            P("row", "col"),
            P("row", "col", "layer"),
        ),
        out_specs=P(("row", "layer"), "col", None, None),
        check_vma=False,
    )
```

```python
import jax
import jax.numpy as jnp
from jax import lax
from jax.experimental import pallas as pl
from jax.experimental.pallas import tpu as pltpu
from jax.sharding import PartitionSpec as P

MESH = pl.DeviceIdType.MESH
BS = 128
SLOTS = 4
DEPTH = SLOTS * BS
MP = 7
NX, NY, NZ = 4, 8, 8
R1 = 224
GROUP = {1: (0, R1), 2: (R1, DEPTH - R1)}
ORDER = (
    ("P", 1, 0, -1), ("X", 0), ("P", 1, -1, 0), ("P", 2, 0, 1), ("X", 1), ("P", 1, 0, 1), ("P", 2, 0, -1), ("X", -1),
    ("P", 2, 0, 2), ("X", 2), ("P", 1, 1, 0), ("P", 2, 0, -2), ("P", 2, -1, 0), ("P", 2, 1, 0), ("P", 1, 0, 2),
    ("P", 1, -1, -1), ("P", 2, -1, -1), ("P", 1, 0, -2), ("P", 1, -1, 1), ("X", -2), ("M", 0), ("P", 2, -1, 1),
    ("P", 1, 2, 0), ("P", 1, 1, -1), ("P", 1, 1, 1), ("P", 2, 1, 1), ("P", 2, 0, 3), ("X", 3), ("P", 2, 1, -1),
    ("M", 1), ("P", 2, -1, 2), ("H", 1, 1, 0), ("C", 0, 1), ("H", 1, -1, 0), ("P", 2, 1, -2), ("P", 2, 1, 2),
    ("P", 2, 2, 0), ("H", 1, 1, 1), ("P", 1, 1, 2), ("P", 2, -1, -2), ("P", 1, 0, 3), ("H", 1, -1, 1), ("P", 2, 2, 1),
    ("C", 1, -1), ("P", 2, 0, -3), ("P", 1, -1, 2), ("X", -3), ("H", 2, 1, 0), ("C", 1, 1), ("H", 2, 1, 1),
    ("P", 1, 1, -2), ("H", 2, -1, 0), ("P", 1, -1, -2), ("P", 2, 2, -1), ("P", 2, -1, 3), ("P", 1, 2, -1),
    ("P", 1, 0, -3), ("P", 1, 2, 1), ("P", 2, 0, 4), ("X", 4), ("P", 1, 0, 4), ("H", 2, -1, 1), ("C", 2, 1),
    ("H", 3, 1, 0), ("C", 2, -1), ("H", 3, -1, 0), ("P", 1, 1, -3), ("P", 2, 2, 2), ("H", 3, 1, 1), ("P", 2, 1, 3),
    ("P", 1, -1, 3), ("H", 3, -1, 1), ("P", 1, 1, 3), ("H", 4, 1, 0), ("P", 2, -1, -3), ("P", 2, 2, -2),
    ("P", 2, 1, -3), ("C", 3, 1), ("P", 1, 2, 2), ("H", 4, 1, 1), ("P", 1, -1, -3), ("C", 3, -1), ("P", 2, 1, 4),
    ("P", 1, 2, -2), ("P", 2, -1, 4), ("C", 4, 1), ("P", 1, -1, 4), ("P", 1, 1, 4), ("Q", 0), ("P", 1, 2, 3),
    ("Q", 3), ("Q", 1), ("P", 2, 2, 3), ("Q", 2), ("P", 2, 2, -3), ("P", 1, 2, 4), ("P", 1, 2, -3), ("P", 2, 2, 4),
)
QUARTERS = 4


def onward(g, a, b):
    out = []
    if g == 1:
        if b == 0:
            if a == 0:
                out += [(1, 0, "x", 1), (-1, 0, "x", -1)]
            if a == 1:
                out += [(2, 0, "x", 1)]
            out += [(a, 1, "y", 1), (a, -1, "y", -1)]
        elif 0 < b < 4:
            out += [(a, b + 1, "y", 1)]
        elif -3 < b < 0:
            out += [(a, b - 1, "y", -1)]
    else:
        if a == 0:
            if b == 0:
                out += [(0, 1, "y", 1), (0, -1, "y", -1)]
            elif 0 < b < 4:
                out += [(0, b + 1, "y", 1)]
            elif -3 < b < 0:
                out += [(0, b - 1, "y", -1)]
            out += [(1, b, "x", 1), (-1, b, "x", -1)]
        elif a == 1:
            out += [(2, b, "x", 1)]
    return out


def kernel(
    a_ref, p_ref, cols_ref, codes_ref, out_ref,
    p_own, p_opp, ps_own, ps_opp, a_all, sums, cols, codes_in, codes_own, codes_opp,
    picks_own, picks_opp, picks_smem_own, picks_smem_opp,
    p_recv, p_send, a_recv, a_send, sib_recv, sib_send, move_send, codes_sem, local_sem,
):
    row, col, layer = lax.axis_index("row"), lax.axis_index("col"), lax.axis_index("layer")
    y, z, core = lax.rem(row, NY), col // 2, lax.rem(col, 2)
    x = (row // NY) * 2 + layer
    turn = 1 - 2 * core
    t = lax.rem(z + 2 * NZ - 4 * layer, NZ)
    q_me = row

    def device(x_, y_, z_, core_):
        return ((x_ // 2) * NY + y_, z_ * 2 + core_, lax.rem(x_, 2))

    def along(axis, way):
        if axis == "x":
            return device(lax.rem(x + NX + turn * way, NX), y, z, core)
        if axis == "y":
            return device(x, lax.rem(y + NY + turn * way, NY), z, core)
        return device(x, y, lax.rem(z + NZ + turn * way, NZ), core)

    sibling = device(x, y, z, 1 - core)
    partner = (row, col, 1 - layer)
    mover = (row, (NZ - 1 - z) * 2 + core, 1 - layer)

    codes_load = pltpu.make_async_copy(codes_ref, codes_in, local_sem.at[4])
    cols_load = pltpu.make_async_copy(cols_ref, cols, local_sem.at[5])
    codes_load.start()
    cols_load.start()

    barrier = pltpu.get_barrier_semaphore()
    greeted = [along(axis, way) for axis in "xyz" for way in (1, -1)] + [sibling, mover]
    for other in greeted:
        pl.semaphore_signal(barrier, inc=1, device_id=other, device_id_type=MESH)
    pl.semaphore_wait(barrier, len(greeted))

    p_land = (p_own, p_opp)
    p_split = (ps_own, ps_opp)
    picks = (picks_own, picks_opp)
    picks_smem = (picks_smem_own, picks_smem_opp)
    codes_land = (codes_own, codes_opp)

    def p_slot(a, b):
        x0 = lax.rem(x + 2 * NX - turn * a, NX)
        y0 = lax.rem(y + 2 * NY - turn * b, NY)
        return (x0 // 2) * NY + y0


    def p_piece(g, a, b):
        lo, size = GROUP[g]
        return p_land[a % 2].at[p_slot(a, b), pl.ds(lo, size)]

    def p_forward(g, a, b, axes="xy"):
        lo, size = GROUP[g]
        src = p_ref.at[pl.ds(lo, size)] if (a, b) == (0, 0) else p_piece(g, a, b)
        copies = []
        for a2, b2, axis, way in onward(g, a, b):
            if axis not in axes:
                continue
            copies.append(
                pltpu.make_async_remote_copy(
                    src_ref=src,
                    dst_ref=p_land[a2 % 2].at[p_slot(a, b), pl.ds(lo, size)],
                    send_sem=p_send.at[g - 1, a2 + 1, b2 + 3],
                    recv_sem=p_recv.at[g - 1, a2 + 1, b2 + 3],
                    device_id=along(axis, way),
                    device_id_type=MESH,
                )
            )
        return copies

    def p_wait(g, a, b):
        here = p_piece(g, a, b)
        pltpu.make_async_remote_copy(
            src_ref=here,
            dst_ref=here,
            send_sem=p_send.at[g - 1, a + 1, b + 3],
            recv_sem=p_recv.at[g - 1, a + 1, b + 3],
            device_id=along("x", 1),
            device_id_type=MESH,
        ).wait_recv()

    def p_convert(a, b, lo, size):
        q = p_slot(a, b)
        value = p_land[a % 2][q, pl.ds(lo, size), :]
        high = value.astype(jnp.bfloat16)
        low = (value - high.astype(jnp.float32)).astype(jnp.bfloat16)
        p_split[a % 2][q, pl.ds(lo, size), pl.ds(0, BS)] = high
        p_split[a % 2][q, pl.ds(lo, size), pl.ds(BS, BS)] = low

    half = DEPTH // 2

    def rows_of(e):
        return jnp.where(e < 4, 2 * e, 8 + 2 * (7 - e))

    def a_half(e, h):
        return a_all.at[rows_of(e) + core, pl.ds(h * half, half)]

    def a_copy(e, h, d, way, src=None):
        return pltpu.make_async_remote_copy(
            src_ref=a_half(e, h) if src is None else src,
            dst_ref=a_half(e, h),
            send_sem=a_send.at[h, (1 - way) // 2, d],
            recv_sem=a_recv.at[h, e],
            device_id=along("z", way),
            device_id_type=MESH,
        )

    def a_wait(e, h):
        a_copy(e, h, 0, 1).wait_recv()

    def sib_copy(e, src=None):
        here = a_all.at[rows_of(e) + core]
        return pltpu.make_async_remote_copy(
            src_ref=here if src is None else src,
            dst_ref=here,
            send_sem=sib_send.at[e],
            recv_sem=sib_recv.at[e],
            device_id=sibling,
            device_id_type=MESH,
        )

    def sib_wait(e):
        there = a_all.at[rows_of(e) + 1 - core]
        pltpu.make_async_remote_copy(
            src_ref=there,
            dst_ref=there,
            send_sem=sib_send.at[e],
            recv_sem=sib_recv.at[e],
            device_id=sibling,
            device_id_type=MESH,
        ).wait_recv()

    def move_copy(h):
        return pltpu.make_async_remote_copy(
            src_ref=a_ref.at[pl.ds(h * half, half)],
            dst_ref=a_half(11 - t, h),
            send_sem=move_send.at[h],
            recv_sem=a_recv.at[h, 11 - t],
            device_id=mover,
            device_id_type=MESH,
        )

    def source(d, way):
        return lax.rem(t + 2 * NZ - turn * way * d, NZ)

    def goes_on(d, way):
        return d < (4 if way == 1 else 3)

    codes_copy = pltpu.make_async_remote_copy(
        src_ref=codes_own,
        dst_ref=codes_opp,
        send_sem=codes_sem.at[0],
        recv_sem=codes_sem.at[1],
        device_id=partner,
        device_id_type=MESH,
    )

    def pick_copy(which):
        return pltpu.make_async_copy(picks[which], picks_smem[which], local_sem.at[2 + which])

    def pick(which):
        codes = [codes_land[which][m] for m in range(MP)]
        for p in range(SLOTS):
            total = jnp.zeros((8, BS), jnp.int32)
            for code in codes:
                for a in range(SLOTS):
                    total += jnp.where(code == a * SLOTS + p, 1 << a, 0)
            picks[which][p] = total
        pick_copy(which).start()

    def combine(e):
        def step(i, carry):
            r = rows_of(e) + i
            strip = 16
            for k in range(BS // strip):
                total = {0: None}
                for n in range(1, 16):
                    a = n.bit_length() - 1
                    part = a_all[r, pl.ds(a * BS + k * strip, strip), :] if n == 1 << a else None
                    total[n] = part if n == 1 << a else total[n - (1 << a)] + total[1 << a]
                    high = total[n].astype(jnp.bfloat16)
                    low = (total[n] - high.astype(jnp.float32)).astype(jnp.bfloat16)
                    sums[r, n, pl.ds(k * strip, strip), :] = high
                    sums[r, n, pl.ds(BS + k * strip, strip), :] = low
            return carry

        lax.fori_loop(0, 2, step, 0)

    def products(which, first, count):
        def step(i, carry):
            r = first + i
            at = 8 * layer + r
            for o in range(SLOTS):
                q = cols[o, at]
                left = jnp.concatenate([sums[8 * which + r, picks_smem[which][p, o, at]] for p in range(SLOTS)], axis=1)
                four = jnp.dot(left, p_split[which][q], preferred_element_type=jnp.float32)
                value = (four[BS:, BS:] + four[:BS, BS:] + four[BS:, :BS]) + four[:BS, :BS]
                where = r * SLOTS + o
                out_ref[where] = value if which == 1 else out_ref[where] + value
            return carry

        lax.fori_loop(0, count, step, 0)

    p_local = pltpu.make_async_copy(p_ref, p_own.at[q_me], local_sem.at[0])
    a_local = pltpu.make_async_copy(a_ref, a_all.at[rows_of(lax.rem(t, 4)) + core], local_sem.at[1])

    @pl.when(t >= 4)
    def _():
        for h in range(2):
            move_copy(h).start()

    for copy in p_forward(1, 0, 0) + p_forward(2, 0, 0, "y"):
        copy.start()

    @pl.when(t < 4)
    def _():
        for h in range(2):
            for way in (1, -1):
                a_copy(t, h, 0, way, a_ref.at[pl.ds(h * half, half)]).start()
        a_local.start()
        sib_copy(t, a_ref).start()

    p_local.start()
    codes_own[...] = jnp.full(codes_own.shape, SLOTS * SLOTS, jnp.int32)
    codes_load.wait()
    codes_own[:, pl.ds(0, SLOTS), pl.ds(0, 16)] = codes_in[...]
    codes_copy.start()
    cols_load.wait()
    pick(0)
    sums[:, 0] = jnp.zeros((16, 2 * BS, BS), jnp.bfloat16)
    p_local.wait()
    p_convert(0, 0, 0, DEPTH)
    codes_copy.wait()
    pick(1)
    for which in range(2):
        pick_copy(which).wait()

    def piece_of_p(g, a, b):
        p_wait(g, a, b)
        for copy in p_forward(g, a, b, "y" if (g, a) == (2, 0) else "xy"):
            copy.start()
        p_convert(a, b, *GROUP[g])

    def across(b):
        for copy in p_forward(2, 0, b, "x"):
            copy.start()

    def moved(h):
        @pl.when(t >= 4)
        def _():
            a_wait(t, h)
            for way in (1, -1):
                a_copy(t, h, 0, way).start()
            if h == 1:
                sib_copy(t).start()

    def hop(d, way, h):
        e = source(d, way)
        a_wait(e, h)
        if goes_on(d, way):
            a_copy(e, h, d, way).start()
        if h == 1:
            sib_copy(e).start()

    def add_up(d, way):
        if d == 0:

            @pl.when(t < 4)
            def _():
                a_local.wait()

        e = source(d, way)
        sib_wait(e)
        combine(e)

    def quarter(i):
        products(1, i * 8 // QUARTERS, 8 // QUARTERS)

    steps = {"P": piece_of_p, "M": moved, "H": hop, "C": add_up, "X": across, "Q": quarter}
    for name, *where in ORDER:
        steps[name](*where)
    products(0, 0, 8)

    for g in (1, 2):
        for a in range(-1, 3):
            for b in range(-3, 5):
                for copy in p_forward(g, a, b):
                    copy.wait_send()

    @pl.when(t >= 4)
    def _():
        for h in range(2):
            move_copy(h).wait_send()

    for d in range(5):
        for way in (1, -1):
            if (d == 4 and way == -1) or (d == 0 and way == -1):
                continue
            e = source(d, way)
            sib_copy(e).wait_send()
    for d in range(4):
        for way in (1, -1):
            if goes_on(d, way):
                for h in range(2):
                    a_copy(source(d, way), h, d, way).wait_send()


def shards(a_blocks, p_blocks, out_columns, pair_codes):
    vmem, smem = pltpu.VMEM, pltpu.SMEM
    dma = pltpu.SemaphoreType.DMA
    f32, bf16 = jnp.float32, jnp.bfloat16
    operands = (
        a_blocks.reshape(DEPTH, BS),
        p_blocks.reshape(DEPTH, BS),
        out_columns.T,
        pair_codes.transpose(2, 1, 0),
    )
    product = pl.pallas_call(
        kernel,
        out_shape=jax.ShapeDtypeStruct((8 * SLOTS, BS, BS), f32),
        in_specs=[
            pl.BlockSpec(memory_space=pltpu.HBM),
            pl.BlockSpec(memory_space=pltpu.HBM),
            pl.BlockSpec(memory_space=pltpu.HBM),
            pl.BlockSpec(memory_space=pltpu.HBM),
        ],
        out_specs=pl.BlockSpec(memory_space=vmem),
        scratch_shapes=[
            vmem((16, DEPTH, BS), f32),
            vmem((16, DEPTH, BS), f32),
            vmem((16, DEPTH, 2 * BS), bf16),
            vmem((16, DEPTH, 2 * BS), bf16),
            vmem((16, DEPTH, BS), f32),
            vmem((16, 16, 2 * BS, BS), bf16),
            smem((SLOTS, 16), jnp.int32),
            vmem((MP, SLOTS, 16), jnp.int32),
            vmem((MP, 8, BS), jnp.int32),
            vmem((MP, 8, BS), jnp.int32),
            vmem((SLOTS, 8, BS), jnp.int32),
            vmem((SLOTS, 8, BS), jnp.int32),
            smem((SLOTS, 8, BS), jnp.int32),
            smem((SLOTS, 8, BS), jnp.int32),
            dma((2, 4, 8)),
            dma((2, 4, 8)),
            dma((2, 8)),
            dma((2, 2, 4)),
            dma((8,)),
            dma((8,)),
            dma((2,)),
            dma((2,)),
            dma((6,)),
        ],
        compiler_params=pltpu.CompilerParams(
            collective_id=0, has_side_effects=True, vmem_limit_bytes=44 * 2**20
        ),
        cost_estimate=pl.CostEstimate(flops=4 * 10**9, bytes_accessed=5 * 2**20, transcendentals=0),
    )(*(pltpu.with_memory_space_constraint(operand, pltpu.HBM) for operand in operands))
    return product.reshape(8, SLOTS, BS, BS)


def solution(mesh):
    return jax.shard_map(
        shards,
        mesh=mesh,
        in_specs=(
            P(("row", "col"), "layer", None, None),
            P(("row", "col"), "layer", None, None),
            P("row", "col"),
            P("row", "col", "layer"),
        ),
        out_specs=P(("row", "layer"), "col", None, None),
        check_vma=False,
    )
```

```python
import jax
import jax.numpy as jnp
from jax import lax
from jax.experimental import pallas as pl
from jax.experimental.pallas import tpu as pltpu
from jax.sharding import PartitionSpec as P

MESH = pl.DeviceIdType.MESH
BS = 128
SLOTS = 4
DEPTH = SLOTS * BS
MP = 7
NX, NY, NZ = 4, 8, 8
R1 = 208
GROUP = {1: (0, R1), 2: (R1, DEPTH - R1)}
ORDER = (
    ("X", 0), ("P", 1, -1, 0), ("P", 2, 0, -1), ("P", 2, 0, 1), ("X", 1), ("P", 1, 0, -1), ("X", -1), ("N",),
    ("P", 2, 0, 2), ("X", 2), ("P", 1, 1, 0), ("P", 2, -1, 0), ("P", 2, 0, -2), ("P", 1, 0, 1), ("M", 0), ("M", 1),
    ("X", -2), ("P", 1, 1, 1), ("P", 2, 1, 0), ("P", 1, -1, 1), ("P", 2, -1, -1), ("P", 1, 0, -2), ("P", 1, 2, 0),
    ("P", 1, 1, -1), ("P", 2, -1, 1), ("P", 2, 1, -1), ("P", 1, -1, -1), ("P", 1, 0, 2), ("P", 2, 1, 1),
    ("H", 1, 1, 0), ("H", 1, -1, 0), ("P", 2, 0, 3), ("X", 3), ("H", 1, -1, 1), ("H", 1, 1, 1), ("P", 2, 1, -2),
    ("C", 0, 1), ("H", 2, 1, 0), ("P", 1, 1, 2), ("H", 2, 1, 1), ("P", 2, 1, 2), ("P", 2, -1, 2), ("H", 2, -1, 0),
    ("P", 1, 0, 3), ("P", 2, 0, -3), ("X", -3), ("P", 1, -1, 2), ("P", 1, 1, -2), ("P", 1, 2, -1), ("C", 1, 1),
    ("P", 2, 2, 0), ("H", 3, 1, 0), ("P", 2, 0, 4), ("H", 2, -1, 1), ("P", 1, 2, 1), ("X", 4), ("C", 1, -1),
    ("P", 1, -1, -2), ("C", 2, 1), ("H", 3, 1, 1), ("P", 2, -1, -2), ("P", 2, 2, 1), ("P", 1, 0, -3), ("P", 2, -1, 3),
    ("H", 3, -1, 0), ("P", 1, 1, 3), ("C", 2, -1), ("H", 3, -1, 1), ("P", 1, -1, 3), ("P", 1, 1, -3), ("P", 2, 1, -3),
    ("H", 4, 1, 0), ("P", 2, 2, 2), ("P", 2, 2, -1), ("C", 3, -1), ("P", 2, 2, -2), ("P", 1, 1, 4), ("H", 4, 1, 1),
    ("C", 3, 1), ("P", 1, 2, 2), ("P", 2, -1, -3), ("P", 1, -1, 4), ("P", 1, 0, 4), ("P", 2, 1, 4), ("P", 2, 1, 3),
    ("P", 1, -1, -3), ("P", 1, 2, -2), ("C", 4, 1), ("P", 2, -1, 4), ("Q", 0), ("Q", 1), ("P", 1, 2, 3), ("Q", 3),
    ("P", 1, 2, -3), ("Q", 2), ("P", 2, 2, 4), ("P", 2, 2, -3), ("P", 1, 2, 4), ("P", 2, 2, 3),
)
QUARTERS = 4


def onward(g, a, b):
    out = []
    if g == 1:
        if b == 0:
            if a == 0:
                out += [(1, 0, "x", 1), (-1, 0, "x", -1)]
            if a == 1:
                out += [(2, 0, "x", 1)]
            out += [(a, 1, "y", 1), (a, -1, "y", -1)]
        elif 0 < b < 4:
            out += [(a, b + 1, "y", 1)]
        elif -3 < b < 0:
            out += [(a, b - 1, "y", -1)]
    else:
        if a == 0:
            if b == 0:
                out += [(0, 1, "y", 1), (0, -1, "y", -1)]
            elif 0 < b < 4:
                out += [(0, b + 1, "y", 1)]
            elif -3 < b < 0:
                out += [(0, b - 1, "y", -1)]
            out += [(1, b, "x", 1), (-1, b, "x", -1)]
        elif a == 1:
            out += [(2, b, "x", 1)]
    return out


def kernel(
    a_ref, p_ref, cols_ref, codes_ref, out_ref,
    p_own, p_opp, ps_own, ps_opp, a_all, sums, cols, codes_in, codes_own, codes_opp,
    picks_own, picks_opp, picks_smem_own, picks_smem_opp,
    passing, p_recv, p_send, a_recv, a_send, sib_recv, sib_send, move_send, pass_sem, codes_sem, local_sem,
):
    row, col, layer = lax.axis_index("row"), lax.axis_index("col"), lax.axis_index("layer")
    y, z, core = lax.rem(row, NY), col // 2, lax.rem(col, 2)
    x = (row // NY) * 2 + layer
    turn = 1 - 2 * core
    t = lax.rem(z + 2 * NZ - 4 * layer, NZ)
    q_me = row

    def device(x_, y_, z_, core_):
        return ((x_ // 2) * NY + y_, z_ * 2 + core_, lax.rem(x_, 2))

    def along(axis, way):
        if axis == "x":
            return device(lax.rem(x + NX + turn * way, NX), y, z, core)
        if axis == "y":
            return device(x, lax.rem(y + NY + turn * way, NY), z, core)
        return device(x, y, lax.rem(z + NZ + turn * way, NZ), core)

    sibling = device(x, y, z, 1 - core)
    partner = (row, col, 1 - layer)
    mover = (row, (NZ - 1 - z) * 2 + core, 1 - layer)
    opposite = (row, (NZ - 1 - z) * 2 + core, layer)

    codes_load = pltpu.make_async_copy(codes_ref, codes_in, local_sem.at[4])
    cols_load = pltpu.make_async_copy(cols_ref, cols, local_sem.at[5])
    codes_load.start()
    cols_load.start()

    barrier = pltpu.get_barrier_semaphore()
    greeted = [along(axis, way) for axis in "xyz" for way in (1, -1)] + [sibling, mover, opposite]
    for other in greeted:
        pl.semaphore_signal(barrier, inc=1, device_id=other, device_id_type=MESH)
    pl.semaphore_wait(barrier, len(greeted))

    p_land = (p_own, p_opp)
    p_split = (ps_own, ps_opp)
    picks = (picks_own, picks_opp)
    picks_smem = (picks_smem_own, picks_smem_opp)
    codes_land = (codes_own, codes_opp)

    def p_slot(a, b):
        x0 = lax.rem(x + 2 * NX - turn * a, NX)
        y0 = lax.rem(y + 2 * NY - turn * b, NY)
        return (x0 // 2) * NY + y0


    def p_piece(g, a, b):
        lo, size = GROUP[g]
        return p_land[a % 2].at[p_slot(a, b), pl.ds(lo, size)]

    def p_forward(g, a, b, axes="xy"):
        lo, size = GROUP[g]
        src = p_ref.at[pl.ds(lo, size)] if (a, b) == (0, 0) else p_piece(g, a, b)
        copies = []
        for a2, b2, axis, way in onward(g, a, b):
            if axis not in axes:
                continue
            copies.append(
                pltpu.make_async_remote_copy(
                    src_ref=src,
                    dst_ref=p_land[a2 % 2].at[p_slot(a, b), pl.ds(lo, size)],
                    send_sem=p_send.at[g - 1, a2 + 1, b2 + 3],
                    recv_sem=p_recv.at[g - 1, a2 + 1, b2 + 3],
                    device_id=along(axis, way),
                    device_id_type=MESH,
                )
            )
        return copies

    def p_wait(g, a, b):
        here = p_piece(g, a, b)
        pltpu.make_async_remote_copy(
            src_ref=here,
            dst_ref=here,
            send_sem=p_send.at[g - 1, a + 1, b + 3],
            recv_sem=p_recv.at[g - 1, a + 1, b + 3],
            device_id=along("x", 1),
            device_id_type=MESH,
        ).wait_recv()

    def p_convert(a, b, lo, size):
        q = p_slot(a, b)
        value = p_land[a % 2][q, pl.ds(lo, size), :]
        high = value.astype(jnp.bfloat16)
        low = (value - high.astype(jnp.float32)).astype(jnp.bfloat16)
        p_split[a % 2][q, pl.ds(lo, size), pl.ds(0, BS)] = high
        p_split[a % 2][q, pl.ds(lo, size), pl.ds(BS, BS)] = low

    half = DEPTH // 2

    def rows_of(e):
        return jnp.where(e < 4, 2 * e, 8 + 2 * (7 - e))

    def a_half(e, h):
        return a_all.at[rows_of(e) + core, pl.ds(h * half, half)]

    def a_copy(e, h, d, way, src=None):
        return pltpu.make_async_remote_copy(
            src_ref=a_half(e, h) if src is None else src,
            dst_ref=a_half(e, h),
            send_sem=a_send.at[h, (1 - way) // 2, d],
            recv_sem=a_recv.at[h, e],
            device_id=along("z", way),
            device_id_type=MESH,
        )

    def a_wait(e, h):
        a_copy(e, h, 0, 1).wait_recv()

    def sib_copy(e, src=None):
        here = a_all.at[rows_of(e) + core]
        return pltpu.make_async_remote_copy(
            src_ref=here if src is None else src,
            dst_ref=here,
            send_sem=sib_send.at[e],
            recv_sem=sib_recv.at[e],
            device_id=sibling,
            device_id_type=MESH,
        )

    def sib_wait(e):
        there = a_all.at[rows_of(e) + 1 - core]
        pltpu.make_async_remote_copy(
            src_ref=there,
            dst_ref=there,
            send_sem=sib_send.at[e],
            recv_sem=sib_recv.at[e],
            device_id=sibling,
            device_id_type=MESH,
        ).wait_recv()

    move_copy = pltpu.make_async_remote_copy(
        src_ref=a_ref.at[pl.ds(0, half)],
        dst_ref=a_half(11 - t, 0),
        send_sem=move_send.at[0],
        recv_sem=a_recv.at[0, 11 - t],
        device_id=mover,
        device_id_type=MESH,
    )
    pass_copy = pltpu.make_async_remote_copy(
        src_ref=a_ref.at[pl.ds(half, half)],
        dst_ref=passing,
        send_sem=pass_sem.at[0],
        recv_sem=pass_sem.at[1],
        device_id=opposite,
        device_id_type=MESH,
    )
    cross_copy = pltpu.make_async_remote_copy(
        src_ref=passing,
        dst_ref=a_half(t + 4, 1),
        send_sem=move_send.at[1],
        recv_sem=a_recv.at[1, t + 4],
        device_id=partner,
        device_id_type=MESH,
    )

    def source(d, way):
        return lax.rem(t + 2 * NZ - turn * way * d, NZ)

    def goes_on(d, way):
        return d < (4 if way == 1 else 3)

    codes_copy = pltpu.make_async_remote_copy(
        src_ref=codes_own,
        dst_ref=codes_opp,
        send_sem=codes_sem.at[0],
        recv_sem=codes_sem.at[1],
        device_id=partner,
        device_id_type=MESH,
    )

    def pick_copy(which):
        return pltpu.make_async_copy(picks[which], picks_smem[which], local_sem.at[2 + which])

    def pick(which):
        codes = [codes_land[which][m] for m in range(MP)]
        for p in range(SLOTS):
            total = jnp.zeros((8, BS), jnp.int32)
            for code in codes:
                for a in range(SLOTS):
                    total += jnp.where(code == a * SLOTS + p, 1 << a, 0)
            picks[which][p] = total
        pick_copy(which).start()

    def combine(e):
        def step(i, carry):
            r = rows_of(e) + i
            strip = 16
            for k in range(BS // strip):
                total = {0: None}
                for n in range(1, 16):
                    a = n.bit_length() - 1
                    part = a_all[r, pl.ds(a * BS + k * strip, strip), :] if n == 1 << a else None
                    total[n] = part if n == 1 << a else total[n - (1 << a)] + total[1 << a]
                    high = total[n].astype(jnp.bfloat16)
                    low = (total[n] - high.astype(jnp.float32)).astype(jnp.bfloat16)
                    sums[r, n, pl.ds(k * strip, strip), :] = high
                    sums[r, n, pl.ds(BS + k * strip, strip), :] = low
            return carry

        lax.fori_loop(0, 2, step, 0)

    def products(which, first, count):
        def step(i, carry):
            r = first + i
            at = 8 * layer + r
            for o in range(SLOTS):
                q = cols[o, at]
                left = jnp.concatenate([sums[8 * which + r, picks_smem[which][p, o, at]] for p in range(SLOTS)], axis=1)
                four = jnp.dot(left, p_split[which][q], preferred_element_type=jnp.float32)
                value = (four[BS:, BS:] + four[:BS, BS:] + four[BS:, :BS]) + four[:BS, :BS]
                where = r * SLOTS + o
                out_ref[where] = value if which == 1 else out_ref[where] + value
            return carry

        lax.fori_loop(0, count, step, 0)

    p_local = pltpu.make_async_copy(p_ref, p_own.at[q_me], local_sem.at[0])
    a_local = pltpu.make_async_copy(a_ref, a_all.at[rows_of(lax.rem(t, 4)) + core], local_sem.at[1])

    @pl.when(t >= 4)
    def _():
        move_copy.start()
        pass_copy.start()

    for copy in p_forward(1, 0, 0) + p_forward(2, 0, 0, "y"):
        copy.start()

    @pl.when(t < 4)
    def _():
        for h in range(2):
            for way in (1, -1):
                a_copy(t, h, 0, way, a_ref.at[pl.ds(h * half, half)]).start()
        a_local.start()
        sib_copy(t, a_ref).start()

    p_local.start()
    codes_own[...] = jnp.full(codes_own.shape, SLOTS * SLOTS, jnp.int32)
    codes_load.wait()
    codes_own[:, pl.ds(0, SLOTS), pl.ds(0, 16)] = codes_in[...]
    codes_copy.start()
    cols_load.wait()
    pick(0)
    sums[:, 0] = jnp.zeros((16, 2 * BS, BS), jnp.bfloat16)
    p_local.wait()
    p_convert(0, 0, 0, DEPTH)
    codes_copy.wait()
    pick(1)
    for which in range(2):
        pick_copy(which).wait()

    def piece_of_p(g, a, b):
        p_wait(g, a, b)
        for copy in p_forward(g, a, b, "y" if (g, a) == (2, 0) else "xy"):
            copy.start()
        p_convert(a, b, *GROUP[g])

    def across(b):
        for copy in p_forward(2, 0, b, "x"):
            copy.start()

    def moved(h):
        @pl.when(t >= 4)
        def _():
            a_wait(t, h)
            for way in (1, -1):
                a_copy(t, h, 0, way).start()
            if h == 1:
                sib_copy(t).start()

    def cross():
        @pl.when(t < 4)
        def _():
            pass_copy.wait_recv()
            cross_copy.start()

    def hop(d, way, h):
        e = source(d, way)
        a_wait(e, h)
        if goes_on(d, way):
            a_copy(e, h, d, way).start()
        if h == 1:
            sib_copy(e).start()

    def add_up(d, way):
        if d == 0:

            @pl.when(t < 4)
            def _():
                a_local.wait()

        e = source(d, way)
        sib_wait(e)
        combine(e)

    def quarter(i):
        products(1, i * 8 // QUARTERS, 8 // QUARTERS)

    steps = {"P": piece_of_p, "M": moved, "H": hop, "C": add_up, "N": cross, "X": across, "Q": quarter}
    for name, *where in ORDER:
        steps[name](*where)
    products(0, 0, 8)

    for g in (1, 2):
        for a in range(-1, 3):
            for b in range(-3, 5):
                for copy in p_forward(g, a, b):
                    copy.wait_send()

    @pl.when(t >= 4)
    def _():
        move_copy.wait_send()
        pass_copy.wait_send()

    @pl.when(t < 4)
    def _():
        cross_copy.wait_send()

    for d in range(5):
        for way in (1, -1):
            if (d == 4 and way == -1) or (d == 0 and way == -1):
                continue
            e = source(d, way)
            sib_copy(e).wait_send()
    for d in range(4):
        for way in (1, -1):
            if goes_on(d, way):
                for h in range(2):
                    a_copy(source(d, way), h, d, way).wait_send()


def shards(a_blocks, p_blocks, out_columns, pair_codes):
    vmem, smem = pltpu.VMEM, pltpu.SMEM
    dma = pltpu.SemaphoreType.DMA
    f32, bf16 = jnp.float32, jnp.bfloat16
    operands = (
        a_blocks.reshape(DEPTH, BS),
        p_blocks.reshape(DEPTH, BS),
        out_columns.T,
        pair_codes.transpose(2, 1, 0),
    )
    product = pl.pallas_call(
        kernel,
        out_shape=jax.ShapeDtypeStruct((8 * SLOTS, BS, BS), f32),
        in_specs=[
            pl.BlockSpec(memory_space=pltpu.HBM),
            pl.BlockSpec(memory_space=pltpu.HBM),
            pl.BlockSpec(memory_space=pltpu.HBM),
            pl.BlockSpec(memory_space=pltpu.HBM),
        ],
        out_specs=pl.BlockSpec(memory_space=vmem),
        scratch_shapes=[
            vmem((16, DEPTH, BS), f32),
            vmem((16, DEPTH, BS), f32),
            vmem((16, DEPTH, 2 * BS), bf16),
            vmem((16, DEPTH, 2 * BS), bf16),
            vmem((16, DEPTH, BS), f32),
            vmem((16, 16, 2 * BS, BS), bf16),
            smem((SLOTS, 16), jnp.int32),
            vmem((MP, SLOTS, 16), jnp.int32),
            vmem((MP, 8, BS), jnp.int32),
            vmem((MP, 8, BS), jnp.int32),
            vmem((SLOTS, 8, BS), jnp.int32),
            vmem((SLOTS, 8, BS), jnp.int32),
            smem((SLOTS, 8, BS), jnp.int32),
            smem((SLOTS, 8, BS), jnp.int32),
            vmem((DEPTH // 2, BS), f32),
            dma((2, 4, 8)),
            dma((2, 4, 8)),
            dma((2, 8)),
            dma((2, 2, 4)),
            dma((8,)),
            dma((8,)),
            dma((2,)),
            dma((2,)),
            dma((2,)),
            dma((6,)),
        ],
        compiler_params=pltpu.CompilerParams(
            collective_id=0, has_side_effects=True, vmem_limit_bytes=44 * 2**20
        ),
        cost_estimate=pl.CostEstimate(flops=4 * 10**9, bytes_accessed=5 * 2**20, transcendentals=0),
    )(*(pltpu.with_memory_space_constraint(operand, pltpu.HBM) for operand in operands))
    return product.reshape(8, SLOTS, BS, BS)


def solution(mesh):
    return jax.shard_map(
        shards,
        mesh=mesh,
        in_specs=(
            P(("row", "col"), "layer", None, None),
            P(("row", "col"), "layer", None, None),
            P("row", "col"),
            P("row", "col", "layer"),
        ),
        out_specs=P(("row", "layer"), "col", None, None),
        check_vma=False,
    )
```

```python
import jax
import jax.numpy as jnp
from jax import lax
from jax.experimental import pallas as pl
from jax.experimental.pallas import tpu as pltpu
from jax.sharding import PartitionSpec as P

MESH = pl.DeviceIdType.MESH
BS = 128
SLOTS = 4
DEPTH = SLOTS * BS
MP = 7
NX, NY, NZ = 4, 8, 8
R1 = 208
GROUP = {1: (0, R1), 2: (R1, DEPTH - R1)}
ORDER = (
    ("X", 0), ("Z",), ("P", 1, 1, 0), ("P", 2, 0, 1), ("P", 1, -1, 0), ("P", 2, 0, -1), ("X", 1), ("P", 1, 0, -1),
    ("X", -1), ("P", 1, 0, 1), ("N",), ("P", 2, 0, 2), ("X", 2), ("P", 1, 1, 1), ("P", 2, 0, -2), ("X", -2),
    ("P", 2, -1, 0), ("M", 0), ("P", 1, 0, -2), ("P", 1, 0, 2), ("P", 2, 1, 0), ("M", 1), ("P", 1, 2, 0),
    ("P", 1, -1, 1), ("P", 2, -1, 1), ("P", 2, -1, -1), ("P", 2, 1, -1), ("H", 1, 1, 0), ("P", 2, 1, 1),
    ("P", 1, 1, -1), ("H", 1, -1, 0), ("P", 2, 1, -2), ("H", 1, 1, 1), ("P", 2, 0, 3), ("X", 3), ("P", 1, 0, -3),
    ("H", 1, -1, 1), ("P", 1, -1, -1), ("P", 1, 1, 2), ("H", 2, 1, 0), ("P", 2, 0, -3), ("C", 0, 1), ("X", -3),
    ("P", 1, 0, 3), ("H", 2, 1, 1), ("C", 1, 1), ("P", 2, 1, 2), ("H", 3, 1, 0), ("P", 1, -1, 2), ("H", 2, -1, 0),
    ("P", 1, 1, -2), ("P", 1, 2, -1), ("H", 2, -1, 1), ("P", 2, -1, 2), ("P", 1, -1, -2), ("P", 2, 0, 4), ("X", 4),
    ("P", 1, 2, 1), ("C", 1, -1), ("C", 2, 1), ("H", 3, 1, 1), ("P", 1, 1, 3), ("P", 2, -1, 3), ("C", 2, -1),
    ("P", 2, -1, -2), ("H", 4, 1, 0), ("P", 2, 2, 0), ("P", 2, 2, -1), ("P", 1, -1, 3), ("P", 2, 2, 1),
    ("P", 1, 1, -3), ("P", 2, 2, -2), ("P", 2, 1, -3), ("H", 3, -1, 0), ("P", 1, 2, 2), ("P", 1, 1, 4),
    ("P", 2, 2, 2), ("H", 4, 1, 1), ("P", 1, 0, 4), ("H", 3, -1, 1), ("C", 3, -1), ("P", 2, 1, 3), ("P", 2, 1, 4),
    ("C", 4, 1), ("P", 1, -1, -3), ("P", 1, -1, 4), ("P", 1, 2, -2), ("P", 1, 2, 3), ("C", 3, 1), ("P", 2, -1, -3),
    ("P", 2, 2, -3), ("P", 2, -1, 4), ("Q", 1), ("Q", 0), ("Q", 3), ("P", 2, 2, 4), ("P", 1, 2, -3), ("P", 2, 2, 3),
    ("Q", 2), ("P", 1, 2, 4),
)
QUARTERS = 4


def onward(g, a, b):
    out = []
    if g == 1:
        if b == 0:
            if a == 0:
                out += [(1, 0, "x", 1), (-1, 0, "x", -1)]
            if a == 1:
                out += [(2, 0, "x", 1)]
            out += [(a, 1, "y", 1), (a, -1, "y", -1)]
        elif 0 < b < 4:
            out += [(a, b + 1, "y", 1)]
        elif -3 < b < 0:
            out += [(a, b - 1, "y", -1)]
    else:
        if a == 0:
            if b == 0:
                out += [(0, 1, "y", 1), (0, -1, "y", -1)]
            elif 0 < b < 4:
                out += [(0, b + 1, "y", 1)]
            elif -3 < b < 0:
                out += [(0, b - 1, "y", -1)]
            out += [(1, b, "x", 1), (-1, b, "x", -1)]
        elif a == 1:
            out += [(2, b, "x", 1)]
    return out


def kernel(
    a_ref, p_ref, cols_ref, codes_ref, out_ref,
    p_own, p_opp, ps_own, ps_opp, a_all, sums, cols, codes_in, codes_own, codes_opp,
    picks_own, picks_opp, picks_smem_own, picks_smem_opp,
    passing, p_recv, p_send, a_recv, a_send, sib_recv, sib_send, move_send, pass_sem, codes_sem, local_sem, plane_ready, line_ready,
):
    row, col, layer = lax.axis_index("row"), lax.axis_index("col"), lax.axis_index("layer")
    y, z, core = lax.rem(row, NY), col // 2, lax.rem(col, 2)
    x = (row // NY) * 2 + layer
    turn = 1 - 2 * core
    t = lax.rem(z + 2 * NZ - 4 * layer, NZ)
    q_me = row

    def device(x_, y_, z_, core_):
        return ((x_ // 2) * NY + y_, z_ * 2 + core_, lax.rem(x_, 2))

    def along(axis, way):
        if axis == "x":
            return device(lax.rem(x + NX + turn * way, NX), y, z, core)
        if axis == "y":
            return device(x, lax.rem(y + NY + turn * way, NY), z, core)
        return device(x, y, lax.rem(z + NZ + turn * way, NZ), core)

    sibling = device(x, y, z, 1 - core)
    partner = (row, col, 1 - layer)
    mover = (row, (NZ - 1 - z) * 2 + core, 1 - layer)
    opposite = (row, (NZ - 1 - z) * 2 + core, layer)

    codes_load = pltpu.make_async_copy(codes_ref, codes_in, local_sem.at[4])
    cols_load = pltpu.make_async_copy(cols_ref, cols, local_sem.at[5])
    codes_load.start()
    cols_load.start()

    barrier = pltpu.get_barrier_semaphore()
    for axis in "xy":
        for way in (1, -1):
            row_, _, layer_ = along(axis, way)
            pl.semaphore_signal(barrier, inc=1, device_id=(row_, z * 2, layer_), device_id_type=MESH)
    for row_, col_, layer_ in (along("z", 1), along("z", -1), mover, opposite):
        pl.semaphore_signal(barrier, inc=1, device_id=(row_, (col_ // 2) * 2 + 1, layer_), device_id_type=MESH)

    @pl.when(core == 0)
    def _():
        pl.semaphore_wait(barrier, 9)
        pl.semaphore_signal(plane_ready, inc=1, device_id=sibling, device_id_type=MESH)

    @pl.when(core == 1)
    def _():
        pl.semaphore_signal(barrier, inc=1, device_id=sibling, device_id_type=MESH)
        pl.semaphore_wait(plane_ready, 1)

    p_land = (p_own, p_opp)
    p_split = (ps_own, ps_opp)
    picks = (picks_own, picks_opp)
    picks_smem = (picks_smem_own, picks_smem_opp)
    codes_land = (codes_own, codes_opp)

    def p_slot(a, b):
        x0 = lax.rem(x + 2 * NX - turn * a, NX)
        y0 = lax.rem(y + 2 * NY - turn * b, NY)
        return (x0 // 2) * NY + y0


    def p_piece(g, a, b):
        lo, size = GROUP[g]
        return p_land[a % 2].at[p_slot(a, b), pl.ds(lo, size)]

    def p_forward(g, a, b, axes="xy"):
        lo, size = GROUP[g]
        src = p_ref.at[pl.ds(lo, size)] if (a, b) == (0, 0) else p_piece(g, a, b)
        copies = []
        for a2, b2, axis, way in onward(g, a, b):
            if axis not in axes:
                continue
            copies.append(
                pltpu.make_async_remote_copy(
                    src_ref=src,
                    dst_ref=p_land[a2 % 2].at[p_slot(a, b), pl.ds(lo, size)],
                    send_sem=p_send.at[g - 1, a2 + 1, b2 + 3],
                    recv_sem=p_recv.at[g - 1, a2 + 1, b2 + 3],
                    device_id=along(axis, way),
                    device_id_type=MESH,
                )
            )
        return copies

    def p_wait(g, a, b):
        here = p_piece(g, a, b)
        pltpu.make_async_remote_copy(
            src_ref=here,
            dst_ref=here,
            send_sem=p_send.at[g - 1, a + 1, b + 3],
            recv_sem=p_recv.at[g - 1, a + 1, b + 3],
            device_id=along("x", 1),
            device_id_type=MESH,
        ).wait_recv()

    def p_convert(a, b, lo, size):
        q = p_slot(a, b)
        value = p_land[a % 2][q, pl.ds(lo, size), :]
        high = value.astype(jnp.bfloat16)
        low = (value - high.astype(jnp.float32)).astype(jnp.bfloat16)
        p_split[a % 2][q, pl.ds(lo, size), pl.ds(0, BS)] = high
        p_split[a % 2][q, pl.ds(lo, size), pl.ds(BS, BS)] = low

    half = DEPTH // 2

    def rows_of(e):
        return jnp.where(e < 4, 2 * e, 8 + 2 * (7 - e))

    def a_half(e, h):
        return a_all.at[rows_of(e) + core, pl.ds(h * half, half)]

    def a_copy(e, h, d, way, src=None):
        return pltpu.make_async_remote_copy(
            src_ref=a_half(e, h) if src is None else src,
            dst_ref=a_half(e, h),
            send_sem=a_send.at[h, (1 - way) // 2, d],
            recv_sem=a_recv.at[h, e],
            device_id=along("z", way),
            device_id_type=MESH,
        )

    def a_wait(e, h):
        a_copy(e, h, 0, 1).wait_recv()

    def sib_copy(e, src=None):
        here = a_all.at[rows_of(e) + core]
        return pltpu.make_async_remote_copy(
            src_ref=here if src is None else src,
            dst_ref=here,
            send_sem=sib_send.at[e],
            recv_sem=sib_recv.at[e],
            device_id=sibling,
            device_id_type=MESH,
        )

    def sib_wait(e):
        there = a_all.at[rows_of(e) + 1 - core]
        pltpu.make_async_remote_copy(
            src_ref=there,
            dst_ref=there,
            send_sem=sib_send.at[e],
            recv_sem=sib_recv.at[e],
            device_id=sibling,
            device_id_type=MESH,
        ).wait_recv()

    move_copy = pltpu.make_async_remote_copy(
        src_ref=a_ref.at[pl.ds(0, half)],
        dst_ref=a_half(11 - t, 0),
        send_sem=move_send.at[0],
        recv_sem=a_recv.at[0, 11 - t],
        device_id=mover,
        device_id_type=MESH,
    )
    pass_copy = pltpu.make_async_remote_copy(
        src_ref=a_ref.at[pl.ds(half, half)],
        dst_ref=passing,
        send_sem=pass_sem.at[0],
        recv_sem=pass_sem.at[1],
        device_id=opposite,
        device_id_type=MESH,
    )
    cross_copy = pltpu.make_async_remote_copy(
        src_ref=passing,
        dst_ref=a_half(t + 4, 1),
        send_sem=move_send.at[1],
        recv_sem=a_recv.at[1, t + 4],
        device_id=partner,
        device_id_type=MESH,
    )

    def source(d, way):
        return lax.rem(t + 2 * NZ - turn * way * d, NZ)

    def goes_on(d, way):
        return d < (4 if way == 1 else 3)

    codes_copy = pltpu.make_async_remote_copy(
        src_ref=codes_own,
        dst_ref=codes_opp,
        send_sem=codes_sem.at[0],
        recv_sem=codes_sem.at[1],
        device_id=partner,
        device_id_type=MESH,
    )

    def pick_copy(which):
        return pltpu.make_async_copy(picks[which], picks_smem[which], local_sem.at[2 + which])

    def pick(which):
        codes = [codes_land[which][m] for m in range(MP)]
        for p in range(SLOTS):
            total = jnp.zeros((8, BS), jnp.int32)
            for code in codes:
                for a in range(SLOTS):
                    total += jnp.where(code == a * SLOTS + p, 1 << a, 0)
            picks[which][p] = total
        pick_copy(which).start()

    def combine(e):
        def step(i, carry):
            r = rows_of(e) + i
            strip = 16
            for k in range(BS // strip):
                total = {0: None}
                for n in range(1, 16):
                    a = n.bit_length() - 1
                    part = a_all[r, pl.ds(a * BS + k * strip, strip), :] if n == 1 << a else None
                    total[n] = part if n == 1 << a else total[n - (1 << a)] + total[1 << a]
                    high = total[n].astype(jnp.bfloat16)
                    low = (total[n] - high.astype(jnp.float32)).astype(jnp.bfloat16)
                    sums[r, n, pl.ds(k * strip, strip), :] = high
                    sums[r, n, pl.ds(BS + k * strip, strip), :] = low
            return carry

        lax.fori_loop(0, 2, step, 0)

    def products(which, first, count):
        def step(i, carry):
            r = first + i
            at = 8 * layer + r
            for o in range(SLOTS):
                q = cols[o, at]
                left = jnp.concatenate([sums[8 * which + r, picks_smem[which][p, o, at]] for p in range(SLOTS)], axis=1)
                four = jnp.dot(left, p_split[which][q], preferred_element_type=jnp.float32)
                value = (four[BS:, BS:] + four[:BS, BS:] + four[BS:, :BS]) + four[:BS, :BS]
                where = r * SLOTS + o
                out_ref[where] = value if which == 1 else out_ref[where] + value
            return carry

        lax.fori_loop(0, count, step, 0)

    p_local = pltpu.make_async_copy(p_ref, p_own.at[q_me], local_sem.at[0])
    a_local = pltpu.make_async_copy(a_ref, a_all.at[rows_of(lax.rem(t, 4)) + core], local_sem.at[1])

    begun = []
    left = []
    now = -1

    def start(*copies):
        for copy in copies:
            copy.start()
            left.append((now, copy.wait_send))

    start(*p_forward(2, 0, 0, "y"), *p_forward(1, 0, 0))

    p_local.start()
    codes_own[...] = jnp.full(codes_own.shape, SLOTS * SLOTS, jnp.int32)
    codes_load.wait()
    codes_own[:, pl.ds(0, SLOTS), pl.ds(0, 16)] = codes_in[...]
    codes_copy.start()
    cols_load.wait()
    pick(0)
    sums[:, 0] = jnp.zeros((16, 2 * BS, BS), jnp.bfloat16)
    p_local.wait()
    p_convert(0, 0, 0, DEPTH)
    pick_copy(0).wait()

    def other_codes():
        codes_copy.wait()
        pick(1)

    def piece_of_p(g, a, b):
        p_wait(g, a, b)
        start(*p_forward(g, a, b, "y" if (g, a) == (2, 0) else "xy"))
        p_convert(a, b, *GROUP[g])

    def across(b):
        start(*p_forward(2, 0, b, "x"))

    def moved(h):
        @pl.when(t >= 4)
        def _():
            a_wait(t, h)
            for way in (1, -1):
                a_copy(t, h, 0, way).start()
            if h == 1:
                sib_copy(t).start()

        for way in (1, -1):
            left.append((now, a_copy(t, h, 0, way).wait_send))
        if h == 1:
            left.append((now, sib_copy(t).wait_send))

    def line():
        @pl.when(core == 1)
        def _():
            pl.semaphore_wait(barrier, 8)
            pl.semaphore_signal(line_ready, inc=1, device_id=sibling, device_id_type=MESH)

        @pl.when(core == 0)
        def _():
            pl.semaphore_wait(line_ready, 1)

        @pl.when(t >= 4)
        def _():
            move_copy.start()
            pass_copy.start()

        @pl.when(t < 4)
        def _():
            for h in range(2):
                for way in (1, -1):
                    a_copy(t, h, 0, way, a_ref.at[pl.ds(h * half, half)]).start()
            a_local.start()
            sib_copy(t, a_ref).start()

    def cross():
        @pl.when(t < 4)
        def _():
            pass_copy.wait_recv()
            cross_copy.start()

    def hop(d, way, h):
        e = source(d, way)
        a_wait(e, h)
        if goes_on(d, way):
            start(a_copy(e, h, d, way))
        if h == 1:
            start(sib_copy(e))

    def add_up(d, way):
        if d == 0:

            @pl.when(t < 4)
            def _():
                a_local.wait()

        e = source(d, way)
        sib_wait(e)
        combine(e)

    def quarter(i):
        if not begun:
            pick_copy(1).wait()
            begun.append(i)
        products(1, i * 8 // QUARTERS, 8 // QUARTERS)

    steps = {"P": piece_of_p, "M": moved, "H": hop, "C": add_up, "N": cross, "Z": line, "X": across, "Q": quarter}
    for now, (name, *where) in enumerate(ORDER):
        if now == 20:
            other_codes()
        if now == len(ORDER) - 3:
            for began, wait in left:
                if began < now - 20:
                    wait()
            left = [entry for entry in left if entry[0] >= now - 20]
        steps[name](*where)
    products(0, 0, 8)

    for _, wait in left:
        wait()

    @pl.when(t >= 4)
    def _():
        move_copy.wait_send()
        pass_copy.wait_send()

    @pl.when(t < 4)
    def _():
        cross_copy.wait_send()


def shards(a_blocks, p_blocks, out_columns, pair_codes):
    vmem, smem = pltpu.VMEM, pltpu.SMEM
    dma = pltpu.SemaphoreType.DMA
    f32, bf16 = jnp.float32, jnp.bfloat16
    operands = (
        a_blocks.reshape(DEPTH, BS),
        p_blocks.reshape(DEPTH, BS),
        out_columns.T,
        pair_codes.transpose(2, 1, 0),
    )
    product = pl.pallas_call(
        kernel,
        out_shape=jax.ShapeDtypeStruct((8 * SLOTS, BS, BS), f32),
        in_specs=[
            pl.BlockSpec(memory_space=pltpu.HBM),
            pl.BlockSpec(memory_space=pltpu.HBM),
            pl.BlockSpec(memory_space=pltpu.HBM),
            pl.BlockSpec(memory_space=pltpu.HBM),
        ],
        out_specs=pl.BlockSpec(memory_space=vmem),
        scratch_shapes=[
            vmem((16, DEPTH, BS), f32),
            vmem((16, DEPTH, BS), f32),
            vmem((16, DEPTH, 2 * BS), bf16),
            vmem((16, DEPTH, 2 * BS), bf16),
            vmem((16, DEPTH, BS), f32),
            vmem((16, 16, 2 * BS, BS), bf16),
            smem((SLOTS, 16), jnp.int32),
            vmem((MP, SLOTS, 16), jnp.int32),
            vmem((MP, 8, BS), jnp.int32),
            vmem((MP, 8, BS), jnp.int32),
            vmem((SLOTS, 8, BS), jnp.int32),
            vmem((SLOTS, 8, BS), jnp.int32),
            smem((SLOTS, 8, BS), jnp.int32),
            smem((SLOTS, 8, BS), jnp.int32),
            vmem((DEPTH // 2, BS), f32),
            dma((2, 4, 8)),
            dma((2, 4, 8)),
            dma((2, 8)),
            dma((2, 2, 4)),
            dma((8,)),
            dma((8,)),
            dma((2,)),
            dma((2,)),
            dma((2,)),
            dma((6,)),
            pltpu.SemaphoreType.REGULAR,
            pltpu.SemaphoreType.REGULAR,
        ],
        compiler_params=pltpu.CompilerParams(
            collective_id=0, has_side_effects=True, vmem_limit_bytes=44 * 2**20
        ),
        cost_estimate=pl.CostEstimate(flops=4 * 10**9, bytes_accessed=5 * 2**20, transcendentals=0),
    )(*(pltpu.with_memory_space_constraint(operand, pltpu.HBM) for operand in operands))
    return product.reshape(8, SLOTS, BS, BS)


def solution(mesh):
    return jax.shard_map(
        shards,
        mesh=mesh,
        in_specs=(
            P(("row", "col"), "layer", None, None),
            P(("row", "col"), "layer", None, None),
            P("row", "col"),
            P("row", "col", "layer"),
        ),
        out_specs=P(("row", "layer"), "col", None, None),
        check_vma=False,
    )
```

```python
import jax
import jax.numpy as jnp
from jax import lax
from jax.experimental import pallas as pl
from jax.experimental.pallas import tpu as pltpu
from jax.sharding import PartitionSpec as P

MESH = pl.DeviceIdType.MESH
BS = 128
SLOTS = 4
DEPTH = SLOTS * BS
MP = 7
NX, NY, NZ = 4, 8, 8
R1 = 208
GROUP = {1: (0, R1), 2: (R1, DEPTH - R1)}
ORDER = (
    ("X", 0), ("Z",), ("P", 1, 1, 0), ("P", 2, 0, 1), ("X", 1), ("P", 1, 0, -1), ("P", 2, 0, -1), ("X", -1),
    ("P", 1, -1, 0), ("N",), ("P", 1, 0, 1), ("P", 2, 0, 2), ("X", 2), ("P", 2, 0, -2), ("X", -2), ("P", 1, 1, 1),
    ("M", 0), ("P", 1, 0, -2), ("P", 2, -1, 0), ("P", 1, 2, 0), ("P", 2, -1, 1), ("P", 1, 0, 2), ("M", 1),
    ("P", 2, 1, 0), ("P", 1, -1, 1), ("P", 2, 1, -1), ("H", 1, -1, 0), ("P", 1, 1, -1), ("P", 2, 1, -2),
    ("H", 1, 1, 0), ("P", 2, 1, 1), ("P", 1, 1, 2), ("H", 1, 1, 1), ("P", 2, -1, -1), ("P", 2, 0, 3), ("X", 3),
    ("P", 1, 0, -3), ("P", 2, 0, -3), ("X", -3), ("H", 2, 1, 0), ("P", 1, -1, -1), ("H", 1, -1, 1), ("P", 1, 2, -1),
    ("C", 0, 1), ("H", 2, 1, 1), ("C", 1, 1), ("P", 1, 1, -2), ("H", 3, 1, 0), ("P", 1, 2, 1), ("P", 1, 0, 3),
    ("P", 1, -1, 2), ("H", 2, -1, 0), ("P", 2, -1, 2), ("H", 2, -1, 1), ("P", 2, 2, 1), ("H", 3, 1, 1),
    ("P", 2, 0, 4), ("X", 4), ("P", 1, 1, 3), ("C", 1, -1), ("C", 2, 1), ("P", 1, -1, -2), ("C", 2, -1),
    ("P", 2, -1, 3), ("P", 2, -1, -2), ("P", 2, 1, 2), ("H", 4, 1, 0), ("P", 2, 2, -1), ("P", 1, 2, 2),
    ("P", 1, -1, 3), ("P", 1, 1, -3), ("H", 3, -1, 0), ("P", 2, 2, -2), ("P", 2, 1, -3), ("P", 1, 2, -2),
    ("H", 3, -1, 1), ("C", 3, -1), ("H", 4, 1, 1), ("P", 1, -1, -3), ("P", 2, 1, 3), ("P", 2, 1, 4), ("P", 1, 1, 4),
    ("C", 3, 1), ("P", 2, -1, -3), ("P", 2, 2, 0), ("P", 1, 2, 3), ("P", 2, -1, 4), ("P", 2, 2, 2), ("P", 1, -1, 4),
    ("C", 4, 1), ("Q", 0), ("P", 1, 2, -3), ("P", 1, 0, 4), ("P", 1, 2, 4), ("Q", 2), ("Q", 1), ("Q", 3),
    ("P", 2, 2, 4), ("P", 2, 2, -3), ("P", 2, 2, 3),
)
QUARTERS = 4


def onward(g, a, b):
    out = []
    if g == 1:
        if b == 0:
            if a == 0:
                out += [(1, 0, "x", 1), (-1, 0, "x", -1)]
            if a == 1:
                out += [(2, 0, "x", 1)]
            out += [(a, 1, "y", 1), (a, -1, "y", -1)]
        elif 0 < b < 4:
            out += [(a, b + 1, "y", 1)]
        elif -3 < b < 0:
            out += [(a, b - 1, "y", -1)]
    else:
        if a == 0:
            if b == 0:
                out += [(0, 1, "y", 1), (0, -1, "y", -1)]
            elif 0 < b < 4:
                out += [(0, b + 1, "y", 1)]
            elif -3 < b < 0:
                out += [(0, b - 1, "y", -1)]
            out += [(1, b, "x", 1), (-1, b, "x", -1)]
        elif a == 1:
            out += [(2, b, "x", 1)]
    return out


def kernel(
    a_ref, p_ref, cols_ref, codes_ref, out_ref,
    p_own, p_opp, ps_own, ps_opp, a_all, sums, cols, codes_in, codes_own, codes_opp,
    picks_own, picks_opp, picks_smem_own, picks_smem_opp,
    passing, p_recv, p_send, a_recv, a_send, sib_recv, sib_send, move_send, pass_sem, codes_sem, local_sem, plane_ready, line_ready,
):
    row, col, layer = lax.axis_index("row"), lax.axis_index("col"), lax.axis_index("layer")
    y, z, core = lax.rem(row, NY), col // 2, lax.rem(col, 2)
    x = (row // NY) * 2 + layer
    turn = 1 - 2 * core
    t = lax.rem(z + 2 * NZ - 4 * layer, NZ)
    q_me = row

    def device(x_, y_, z_, core_):
        return ((x_ // 2) * NY + y_, z_ * 2 + core_, lax.rem(x_, 2))

    def along(axis, way):
        if axis == "x":
            return device(lax.rem(x + NX + turn * way, NX), y, z, core)
        if axis == "y":
            return device(x, lax.rem(y + NY + turn * way, NY), z, core)
        return device(x, y, lax.rem(z + NZ + turn * way, NZ), core)

    sibling = device(x, y, z, 1 - core)
    partner = (row, col, 1 - layer)
    mover = (row, (NZ - 1 - z) * 2 + core, 1 - layer)
    opposite = (row, (NZ - 1 - z) * 2 + core, layer)

    codes_load = pltpu.make_async_copy(codes_ref, codes_in, local_sem.at[4])
    cols_load = pltpu.make_async_copy(cols_ref, cols, local_sem.at[5])
    codes_load.start()
    cols_load.start()

    barrier = pltpu.get_barrier_semaphore()
    for axis in "xy":
        for way in (1, -1):
            row_, _, layer_ = along(axis, way)
            pl.semaphore_signal(barrier, inc=1, device_id=(row_, z * 2, layer_), device_id_type=MESH)
    for row_, col_, layer_ in (along("z", 1), along("z", -1), mover, opposite):
        pl.semaphore_signal(barrier, inc=1, device_id=(row_, (col_ // 2) * 2 + 1, layer_), device_id_type=MESH)

    @pl.when(core == 0)
    def _():
        pl.semaphore_wait(barrier, 9)
        pl.semaphore_signal(plane_ready, inc=1, device_id=sibling, device_id_type=MESH)

    @pl.when(core == 1)
    def _():
        pl.semaphore_signal(barrier, inc=1, device_id=sibling, device_id_type=MESH)
        pl.semaphore_wait(plane_ready, 1)

    p_land = (p_own, p_opp)
    p_split = (ps_own, ps_opp)
    picks = (picks_own, picks_opp)
    picks_smem = (picks_smem_own, picks_smem_opp)
    codes_land = (codes_own, codes_opp)

    def p_slot(a, b):
        x0 = lax.rem(x + 2 * NX - turn * a, NX)
        y0 = lax.rem(y + 2 * NY - turn * b, NY)
        return (x0 // 2) * NY + y0


    def p_piece(g, a, b):
        lo, size = GROUP[g]
        return p_land[a % 2].at[p_slot(a, b), pl.ds(lo, size)]

    def p_forward(g, a, b, axes="xy"):
        lo, size = GROUP[g]
        src = p_ref.at[pl.ds(lo, size)] if (a, b) == (0, 0) else p_piece(g, a, b)
        copies = []
        for a2, b2, axis, way in onward(g, a, b):
            if axis not in axes:
                continue
            copies.append(
                pltpu.make_async_remote_copy(
                    src_ref=src,
                    dst_ref=p_land[a2 % 2].at[p_slot(a, b), pl.ds(lo, size)],
                    send_sem=p_send.at[g - 1, a2 + 1, b2 + 3],
                    recv_sem=p_recv.at[g - 1, a2 + 1, b2 + 3],
                    device_id=along(axis, way),
                    device_id_type=MESH,
                )
            )
        return copies

    def p_wait(g, a, b):
        here = p_piece(g, a, b)
        pltpu.make_async_remote_copy(
            src_ref=here,
            dst_ref=here,
            send_sem=p_send.at[g - 1, a + 1, b + 3],
            recv_sem=p_recv.at[g - 1, a + 1, b + 3],
            device_id=along("x", 1),
            device_id_type=MESH,
        ).wait_recv()

    def p_convert(a, b, lo, size):
        q = p_slot(a, b)
        value = p_land[a % 2][q, pl.ds(lo, size), :]
        high = value.astype(jnp.bfloat16)
        low = (value - high.astype(jnp.float32)).astype(jnp.bfloat16)
        p_split[a % 2][q, pl.ds(lo, size), pl.ds(0, BS)] = high
        p_split[a % 2][q, pl.ds(lo, size), pl.ds(BS, BS)] = low

    half = DEPTH // 2

    def rows_of(e):
        return jnp.where(e < 4, 2 * e, 8 + 2 * (7 - e))

    def a_half(e, h):
        return a_all.at[rows_of(e) + core, pl.ds(h * half, half)]

    def a_copy(e, h, d, way, src=None):
        return pltpu.make_async_remote_copy(
            src_ref=a_half(e, h) if src is None else src,
            dst_ref=a_half(e, h),
            send_sem=a_send.at[h, (1 - way) // 2, d],
            recv_sem=a_recv.at[h, e],
            device_id=along("z", way),
            device_id_type=MESH,
        )

    def a_wait(e, h):
        a_copy(e, h, 0, 1).wait_recv()

    def sib_copy(e, src=None):
        here = a_all.at[rows_of(e) + core]
        return pltpu.make_async_remote_copy(
            src_ref=here if src is None else src,
            dst_ref=here,
            send_sem=sib_send.at[e],
            recv_sem=sib_recv.at[e],
            device_id=sibling,
            device_id_type=MESH,
        )

    def sib_wait(e):
        there = a_all.at[rows_of(e) + 1 - core]
        pltpu.make_async_remote_copy(
            src_ref=there,
            dst_ref=there,
            send_sem=sib_send.at[e],
            recv_sem=sib_recv.at[e],
            device_id=sibling,
            device_id_type=MESH,
        ).wait_recv()

    move_copy = pltpu.make_async_remote_copy(
        src_ref=a_ref.at[pl.ds(0, half)],
        dst_ref=a_half(11 - t, 0),
        send_sem=move_send.at[0],
        recv_sem=a_recv.at[0, 11 - t],
        device_id=mover,
        device_id_type=MESH,
    )
    pass_copy = pltpu.make_async_remote_copy(
        src_ref=a_ref.at[pl.ds(half, half)],
        dst_ref=passing,
        send_sem=pass_sem.at[0],
        recv_sem=pass_sem.at[1],
        device_id=opposite,
        device_id_type=MESH,
    )
    cross_copy = pltpu.make_async_remote_copy(
        src_ref=passing,
        dst_ref=a_half(t + 4, 1),
        send_sem=move_send.at[1],
        recv_sem=a_recv.at[1, t + 4],
        device_id=partner,
        device_id_type=MESH,
    )

    def source(d, way):
        return lax.rem(t + 2 * NZ - turn * way * d, NZ)

    def goes_on(d, way):
        return d < (4 if way == 1 else 3)

    codes_copy = pltpu.make_async_remote_copy(
        src_ref=codes_own,
        dst_ref=codes_opp,
        send_sem=codes_sem.at[0],
        recv_sem=codes_sem.at[1],
        device_id=partner,
        device_id_type=MESH,
    )

    def pick_copy(which):
        return pltpu.make_async_copy(picks[which], picks_smem[which], local_sem.at[2 + which])

    def pick(which):
        codes = [codes_land[which][m] for m in range(MP)]
        for p in range(SLOTS):
            total = jnp.zeros((8, BS), jnp.int32)
            for code in codes:
                for a in range(SLOTS):
                    total += jnp.where(code == a * SLOTS + p, 1 << a, 0)
            picks[which][p] = total
        pick_copy(which).start()

    def combine(e):
        def step(i, carry):
            r = rows_of(e) + i
            strip = 16
            for k in range(BS // strip):
                total = {0: None}
                for n in range(1, 16):
                    a = n.bit_length() - 1
                    part = a_all[r, pl.ds(a * BS + k * strip, strip), :] if n == 1 << a else None
                    total[n] = part if n == 1 << a else total[n - (1 << a)] + total[1 << a]
                    high = total[n].astype(jnp.bfloat16)
                    low = (total[n] - high.astype(jnp.float32)).astype(jnp.bfloat16)
                    sums[r, n, pl.ds(k * strip, strip), :] = high
                    sums[r, n, pl.ds(BS + k * strip, strip), :] = low
            return carry

        lax.fori_loop(0, 2, step, 0)

    def products(which, first, count):
        def step(i, carry):
            for j in range(2):
                r = first + 2 * i + j
                at = 8 * layer + r
                for o in range(SLOTS):
                    q = cols[o, at]
                    left = jnp.concatenate([sums[8 * which + r, picks_smem[which][p, o, at]] for p in range(SLOTS)], axis=1)
                    four = jnp.dot(left, p_split[which][q], preferred_element_type=jnp.float32)
                    value = (four[BS:, BS:] + four[:BS, BS:] + four[BS:, :BS]) + four[:BS, :BS]
                    where = r * SLOTS + o
                    out_ref[where] = value if which == 1 else out_ref[where] + value
            return carry

        lax.fori_loop(0, count // 2, step, 0)

    p_local = pltpu.make_async_copy(p_ref, p_own.at[q_me], local_sem.at[0])
    a_local = pltpu.make_async_copy(a_ref, a_all.at[rows_of(lax.rem(t, 4)) + core], local_sem.at[1])

    begun = []
    left = []
    now = -1

    def start(*copies):
        for copy in copies:
            copy.start()
            left.append((now, copy.wait_send))

    start(*p_forward(2, 0, 0, "y"), *p_forward(1, 0, 0))

    p_local.start()
    codes_own[...] = jnp.full(codes_own.shape, SLOTS * SLOTS, jnp.int32)
    codes_load.wait()
    codes_own[:, pl.ds(0, SLOTS), pl.ds(0, 16)] = codes_in[...]
    codes_copy.start()
    cols_load.wait()
    pick(0)
    sums[:, 0] = jnp.zeros((16, 2 * BS, BS), jnp.bfloat16)
    p_local.wait()
    p_convert(0, 0, 0, DEPTH)
    pick_copy(0).wait()

    def other_codes():
        codes_copy.wait()
        pick(1)

    def piece_of_p(g, a, b):
        p_wait(g, a, b)
        start(*p_forward(g, a, b, "y" if (g, a) == (2, 0) else "xy"))
        p_convert(a, b, *GROUP[g])

    def across(b):
        start(*p_forward(2, 0, b, "x"))

    def moved(h):
        @pl.when(t >= 4)
        def _():
            a_wait(t, h)
            for way in (1, -1):
                a_copy(t, h, 0, way).start()
            if h == 1:
                sib_copy(t).start()

        for way in (1, -1):
            left.append((now, a_copy(t, h, 0, way).wait_send))
        if h == 1:
            left.append((now, sib_copy(t).wait_send))

    def line():
        @pl.when(core == 1)
        def _():
            pl.semaphore_wait(barrier, 8)
            pl.semaphore_signal(line_ready, inc=1, device_id=sibling, device_id_type=MESH)

        @pl.when(core == 0)
        def _():
            pl.semaphore_wait(line_ready, 1)

        @pl.when(t >= 4)
        def _():
            move_copy.start()
            pass_copy.start()

        @pl.when(t < 4)
        def _():
            for h in range(2):
                for way in (1, -1):
                    a_copy(t, h, 0, way, a_ref.at[pl.ds(h * half, half)]).start()
            a_local.start()
            sib_copy(t, a_ref).start()

    def cross():
        @pl.when(t < 4)
        def _():
            pass_copy.wait_recv()
            cross_copy.start()

    def hop(d, way, h):
        e = source(d, way)
        a_wait(e, h)
        if goes_on(d, way):
            start(a_copy(e, h, d, way))
        if h == 1:
            start(sib_copy(e))

    def add_up(d, way):
        if d == 0:

            @pl.when(t < 4)
            def _():
                a_local.wait()

        e = source(d, way)
        sib_wait(e)
        combine(e)

    def quarter(i):
        if not begun:
            pick_copy(1).wait()
            begun.append(i)
        products(1, i * 8 // QUARTERS, 8 // QUARTERS)

    steps = {"P": piece_of_p, "M": moved, "H": hop, "C": add_up, "N": cross, "Z": line, "X": across, "Q": quarter}
    for now, (name, *where) in enumerate(ORDER):
        if now == 20:
            other_codes()
        if now == len(ORDER) - 3:
            for began, wait in left:
                if began < now - 20:
                    wait()
            left = [entry for entry in left if entry[0] >= now - 20]
        steps[name](*where)
    products(0, 0, 8)

    for _, wait in left:
        wait()

    @pl.when(t >= 4)
    def _():
        move_copy.wait_send()
        pass_copy.wait_send()

    @pl.when(t < 4)
    def _():
        cross_copy.wait_send()


def shards(a_blocks, p_blocks, out_columns, pair_codes):
    vmem, smem = pltpu.VMEM, pltpu.SMEM
    dma = pltpu.SemaphoreType.DMA
    f32, bf16 = jnp.float32, jnp.bfloat16
    operands = (
        a_blocks.reshape(DEPTH, BS),
        p_blocks.reshape(DEPTH, BS),
        out_columns.T,
        pair_codes.transpose(2, 1, 0),
    )
    product = pl.pallas_call(
        kernel,
        out_shape=jax.ShapeDtypeStruct((8 * SLOTS, BS, BS), f32),
        in_specs=[
            pl.BlockSpec(memory_space=pltpu.HBM),
            pl.BlockSpec(memory_space=pltpu.HBM),
            pl.BlockSpec(memory_space=pltpu.HBM),
            pl.BlockSpec(memory_space=pltpu.HBM),
        ],
        out_specs=pl.BlockSpec(memory_space=vmem),
        scratch_shapes=[
            vmem((16, DEPTH, BS), f32),
            vmem((16, DEPTH, BS), f32),
            vmem((16, DEPTH, 2 * BS), bf16),
            vmem((16, DEPTH, 2 * BS), bf16),
            vmem((16, DEPTH, BS), f32),
            vmem((16, 16, 2 * BS, BS), bf16),
            smem((SLOTS, 16), jnp.int32),
            vmem((MP, SLOTS, 16), jnp.int32),
            vmem((MP, 8, BS), jnp.int32),
            vmem((MP, 8, BS), jnp.int32),
            vmem((SLOTS, 8, BS), jnp.int32),
            vmem((SLOTS, 8, BS), jnp.int32),
            smem((SLOTS, 8, BS), jnp.int32),
            smem((SLOTS, 8, BS), jnp.int32),
            vmem((DEPTH // 2, BS), f32),
            dma((2, 4, 8)),
            dma((2, 4, 8)),
            dma((2, 8)),
            dma((2, 2, 4)),
            dma((8,)),
            dma((8,)),
            dma((2,)),
            dma((2,)),
            dma((2,)),
            dma((6,)),
            pltpu.SemaphoreType.REGULAR,
            pltpu.SemaphoreType.REGULAR,
        ],
        compiler_params=pltpu.CompilerParams(
            collective_id=0, has_side_effects=True, vmem_limit_bytes=44 * 2**20
        ),
        cost_estimate=pl.CostEstimate(flops=4 * 10**9, bytes_accessed=5 * 2**20, transcendentals=0),
    )(*(pltpu.with_memory_space_constraint(operand, pltpu.HBM) for operand in operands))
    return product.reshape(8, SLOTS, BS, BS)


def solution(mesh):
    return jax.shard_map(
        shards,
        mesh=mesh,
        in_specs=(
            P(("row", "col"), "layer", None, None),
            P(("row", "col"), "layer", None, None),
            P("row", "col"),
            P("row", "col", "layer"),
        ),
        out_specs=P(("row", "layer"), "col", None, None),
        check_vma=False,
    )
```

```python
import jax
import jax.numpy as jnp
from jax import lax
from jax.experimental import pallas as pl
from jax.experimental.pallas import tpu as pltpu
from jax.sharding import PartitionSpec as P

MESH = pl.DeviceIdType.MESH
BS = 128
SLOTS = 4
DEPTH = SLOTS * BS
MP = 7
NX, NY, NZ = 4, 8, 8
R1 = 208
GROUP = {1: (0, R1), 2: (R1, DEPTH - R1)}
ORDER = (
    ("X", 0), ("Z",), ("P", 1, 1, 0), ("P", 2, 0, 1), ("X", 1), ("P", 1, 0, -1), ("P", 2, 0, -1), ("X", -1),
    ("P", 1, -1, 0), ("N",), ("P", 1, 0, 1), ("P", 2, 0, 2), ("X", 2), ("P", 2, 0, -2), ("X", -2), ("P", 1, 1, 1),
    ("P", 1, 0, -2), ("P", 1, 2, 0), ("P", 2, -1, 0), ("M", 0), ("P", 1, 0, 2), ("P", 2, -1, 1), ("P", 2, 1, 1),
    ("P", 2, 1, 0), ("P", 1, -1, 1), ("P", 2, 1, -1), ("M", 1), ("H", 1, -1, 0), ("P", 1, 1, -1), ("H", 1, 1, 0),
    ("P", 2, 1, -2), ("H", 1, 1, 1), ("P", 1, 1, 2), ("P", 2, -1, -1), ("P", 2, 0, 3), ("X", 3), ("P", 1, 0, -3),
    ("P", 2, 0, -3), ("X", -3), ("H", 2, 1, 0), ("P", 1, -1, -1), ("H", 1, -1, 1), ("P", 1, 2, -1), ("C", 0, 1),
    ("H", 2, 1, 1), ("P", 1, 1, -2), ("C", 1, 1), ("H", 3, 1, 0), ("P", 2, -1, 2), ("P", 1, 2, 1), ("H", 2, -1, 0),
    ("P", 1, 0, 3), ("P", 1, -1, 2), ("H", 2, -1, 1), ("H", 3, 1, 1), ("P", 2, 0, 4), ("P", 2, 2, 1), ("X", 4),
    ("P", 1, 1, 3), ("C", 1, -1), ("C", 2, 1), ("P", 1, -1, -2), ("C", 2, -1), ("P", 2, 1, 2), ("P", 2, -1, 3),
    ("P", 2, -1, -2), ("H", 4, 1, 0), ("P", 2, 2, -1), ("P", 1, 2, 2), ("P", 1, -1, 3), ("P", 1, 1, -3),
    ("P", 1, 1, 4), ("H", 3, -1, 0), ("P", 2, 2, -2), ("P", 2, 1, -3), ("P", 1, 2, -2), ("H", 3, -1, 1),
    ("H", 4, 1, 1), ("C", 3, -1), ("P", 1, -1, -3), ("P", 2, 1, 3), ("P", 2, 1, 4), ("C", 3, 1), ("P", 1, 2, 3),
    ("P", 2, 2, 0), ("P", 2, -1, -3), ("P", 1, -1, 4), ("P", 2, -1, 4), ("O", 1, 1), ("P", 2, 2, 2), ("C", 4, 1),
    ("P", 1, 2, -3), ("O", 1, -1), ("O", 0, 1), ("O", 2, 1), ("O", 2, -1), ("O", 3, 1), ("O", 3, -1), ("O", 4, 1),
    ("P", 1, 0, 4), ("P", 2, 2, 4), ("P", 1, 2, 4), ("P", 2, 2, -3), ("P", 2, 2, 3),
)


def onward(g, a, b):
    out = []
    if g == 1:
        if b == 0:
            if a == 0:
                out += [(1, 0, "x", 1), (-1, 0, "x", -1)]
            if a == 1:
                out += [(2, 0, "x", 1)]
            out += [(a, 1, "y", 1), (a, -1, "y", -1)]
        elif 0 < b < 4:
            out += [(a, b + 1, "y", 1)]
        elif -3 < b < 0:
            out += [(a, b - 1, "y", -1)]
    else:
        if a == 0:
            if b == 0:
                out += [(0, 1, "y", 1), (0, -1, "y", -1)]
            elif 0 < b < 4:
                out += [(0, b + 1, "y", 1)]
            elif -3 < b < 0:
                out += [(0, b - 1, "y", -1)]
            out += [(1, b, "x", 1), (-1, b, "x", -1)]
        elif a == 1:
            out += [(2, b, "x", 1)]
    return out


def kernel(
    a_ref, p_ref, cols_ref, codes_ref, out_ref,
    p_own, p_opp, ps_own, ps_opp, a_all, sums, cols, codes_in, codes_own, codes_opp,
    picks_own, picks_opp, picks_smem_own, picks_smem_opp,
    passing, p_recv, p_send, a_recv, a_send, sib_recv, sib_send, move_send, pass_sem, codes_sem, local_sem, plane_ready, line_ready,
):
    row, col, layer = lax.axis_index("row"), lax.axis_index("col"), lax.axis_index("layer")
    y, z, core = lax.rem(row, NY), col // 2, lax.rem(col, 2)
    x = (row // NY) * 2 + layer
    turn = 1 - 2 * core
    t = lax.rem(z + 2 * NZ - 4 * layer, NZ)
    q_me = row

    def device(x_, y_, z_, core_):
        return ((x_ // 2) * NY + y_, z_ * 2 + core_, lax.rem(x_, 2))

    def along(axis, way):
        if axis == "x":
            return device(lax.rem(x + NX + turn * way, NX), y, z, core)
        if axis == "y":
            return device(x, lax.rem(y + NY + turn * way, NY), z, core)
        return device(x, y, lax.rem(z + NZ + turn * way, NZ), core)

    sibling = device(x, y, z, 1 - core)
    partner = (row, col, 1 - layer)
    mover = (row, (NZ - 1 - z) * 2 + core, 1 - layer)
    opposite = (row, (NZ - 1 - z) * 2 + core, layer)

    codes_load = pltpu.make_async_copy(codes_ref, codes_in, local_sem.at[4])
    cols_load = pltpu.make_async_copy(cols_ref, cols, local_sem.at[5])
    codes_load.start()
    cols_load.start()

    barrier = pltpu.get_barrier_semaphore()
    for axis in "xy":
        for way in (1, -1):
            row_, _, layer_ = along(axis, way)
            pl.semaphore_signal(barrier, inc=1, device_id=(row_, z * 2, layer_), device_id_type=MESH)
    for row_, col_, layer_ in (along("z", 1), along("z", -1), mover, opposite):
        pl.semaphore_signal(barrier, inc=1, device_id=(row_, (col_ // 2) * 2 + 1, layer_), device_id_type=MESH)

    @pl.when(core == 0)
    def _():
        pl.semaphore_wait(barrier, 9)
        pl.semaphore_signal(plane_ready, inc=1, device_id=sibling, device_id_type=MESH)

    @pl.when(core == 1)
    def _():
        pl.semaphore_signal(barrier, inc=1, device_id=sibling, device_id_type=MESH)
        pl.semaphore_wait(plane_ready, 1)

    p_land = (p_own, p_opp)
    p_split = (ps_own, ps_opp)
    picks = (picks_own, picks_opp)
    picks_smem = (picks_smem_own, picks_smem_opp)
    codes_land = (codes_own, codes_opp)

    def p_slot(a, b):
        x0 = lax.rem(x + 2 * NX - turn * a, NX)
        y0 = lax.rem(y + 2 * NY - turn * b, NY)
        return (x0 // 2) * NY + y0


    def p_piece(g, a, b):
        lo, size = GROUP[g]
        return p_land[a % 2].at[p_slot(a, b), pl.ds(lo, size)]

    def p_forward(g, a, b, axes="xy"):
        lo, size = GROUP[g]
        src = p_ref.at[pl.ds(lo, size)] if (a, b) == (0, 0) else p_piece(g, a, b)
        copies = []
        for a2, b2, axis, way in onward(g, a, b):
            if axis not in axes:
                continue
            copies.append(
                pltpu.make_async_remote_copy(
                    src_ref=src,
                    dst_ref=p_land[a2 % 2].at[p_slot(a, b), pl.ds(lo, size)],
                    send_sem=p_send.at[g - 1, a2 + 1, b2 + 3],
                    recv_sem=p_recv.at[g - 1, a2 + 1, b2 + 3],
                    device_id=along(axis, way),
                    device_id_type=MESH,
                )
            )
        return copies

    def p_wait(g, a, b):
        here = p_piece(g, a, b)
        pltpu.make_async_remote_copy(
            src_ref=here,
            dst_ref=here,
            send_sem=p_send.at[g - 1, a + 1, b + 3],
            recv_sem=p_recv.at[g - 1, a + 1, b + 3],
            device_id=along("x", 1),
            device_id_type=MESH,
        ).wait_recv()

    def p_convert(a, b, lo, size):
        q = p_slot(a, b)
        value = p_land[a % 2][q, pl.ds(lo, size), :]
        high = value.astype(jnp.bfloat16)
        low = (value - high.astype(jnp.float32)).astype(jnp.bfloat16)
        p_split[a % 2][q, pl.ds(lo, size), pl.ds(0, BS)] = high
        p_split[a % 2][q, pl.ds(lo, size), pl.ds(BS, BS)] = low

    half = DEPTH // 2

    def rows_of(e):
        return jnp.where(e < 4, 2 * e, 8 + 2 * (7 - e))

    def a_half(e, h):
        return a_all.at[rows_of(e) + core, pl.ds(h * half, half)]

    def a_copy(e, h, d, way, src=None):
        return pltpu.make_async_remote_copy(
            src_ref=a_half(e, h) if src is None else src,
            dst_ref=a_half(e, h),
            send_sem=a_send.at[h, (1 - way) // 2, d],
            recv_sem=a_recv.at[h, e],
            device_id=along("z", way),
            device_id_type=MESH,
        )

    def a_wait(e, h):
        a_copy(e, h, 0, 1).wait_recv()

    def sib_copy(e, src=None):
        here = a_all.at[rows_of(e) + core]
        return pltpu.make_async_remote_copy(
            src_ref=here if src is None else src,
            dst_ref=here,
            send_sem=sib_send.at[e],
            recv_sem=sib_recv.at[e],
            device_id=sibling,
            device_id_type=MESH,
        )

    def sib_wait(e):
        there = a_all.at[rows_of(e) + 1 - core]
        pltpu.make_async_remote_copy(
            src_ref=there,
            dst_ref=there,
            send_sem=sib_send.at[e],
            recv_sem=sib_recv.at[e],
            device_id=sibling,
            device_id_type=MESH,
        ).wait_recv()

    move_copy = pltpu.make_async_remote_copy(
        src_ref=a_ref.at[pl.ds(0, half)],
        dst_ref=a_half(11 - t, 0),
        send_sem=move_send.at[0],
        recv_sem=a_recv.at[0, 11 - t],
        device_id=mover,
        device_id_type=MESH,
    )
    pass_copy = pltpu.make_async_remote_copy(
        src_ref=a_ref.at[pl.ds(half, half)],
        dst_ref=passing,
        send_sem=pass_sem.at[0],
        recv_sem=pass_sem.at[1],
        device_id=opposite,
        device_id_type=MESH,
    )
    cross_copy = pltpu.make_async_remote_copy(
        src_ref=passing,
        dst_ref=a_half(t + 4, 1),
        send_sem=move_send.at[1],
        recv_sem=a_recv.at[1, t + 4],
        device_id=partner,
        device_id_type=MESH,
    )

    def source(d, way):
        return lax.rem(t + 2 * NZ - turn * way * d, NZ)

    def goes_on(d, way):
        return d < (4 if way == 1 else 3)

    codes_copy = pltpu.make_async_remote_copy(
        src_ref=codes_own,
        dst_ref=codes_opp,
        send_sem=codes_sem.at[0],
        recv_sem=codes_sem.at[1],
        device_id=partner,
        device_id_type=MESH,
    )

    def pick_copy(which):
        return pltpu.make_async_copy(picks[which], picks_smem[which], local_sem.at[2 + which])

    def pick(which):
        codes = [codes_land[which][m] for m in range(MP)]
        for p in range(SLOTS):
            total = jnp.zeros((8, BS), jnp.int32)
            for code in codes:
                for a in range(SLOTS):
                    total += jnp.where(code == a * SLOTS + p, 1 << a, 0)
            picks[which][p] = total
        pick_copy(which).start()

    def combine(e):
        def step(i, carry):
            r = rows_of(e) + i
            strip = 16
            for k in range(BS // strip):
                total = {0: None}
                for n in range(1, 16):
                    a = n.bit_length() - 1
                    part = a_all[r, pl.ds(a * BS + k * strip, strip), :] if n == 1 << a else None
                    total[n] = part if n == 1 << a else total[n - (1 << a)] + total[1 << a]
                    high = total[n].astype(jnp.bfloat16)
                    low = (total[n] - high.astype(jnp.float32)).astype(jnp.bfloat16)
                    sums[r, n, pl.ds(k * strip, strip), :] = high
                    sums[r, n, pl.ds(BS + k * strip, strip), :] = low
            return carry

        lax.fori_loop(0, 2, step, 0)

    def products(which, first, count):
        def step(i, carry):
            r = first + i
            at = 8 * layer + r
            for o in range(SLOTS):
                q = cols[o, at]
                left = jnp.concatenate([sums[8 * which + r, picks_smem[which][p, o, at]] for p in range(SLOTS)], axis=1)
                four = jnp.dot(left, p_split[which][q], preferred_element_type=jnp.float32)
                value = (four[BS:, BS:] + four[:BS, BS:] + four[BS:, :BS]) + four[:BS, :BS]
                where = r * SLOTS + o
                out_ref[where] = value if which == 1 else out_ref[where] + value
            return carry

        lax.fori_loop(0, count, step, 0)

    p_local = pltpu.make_async_copy(p_ref, p_own.at[q_me], local_sem.at[0])
    a_local = pltpu.make_async_copy(a_ref, a_all.at[rows_of(lax.rem(t, 4)) + core], local_sem.at[1])

    begun = []
    left = []
    now = -1

    def start(*copies):
        for copy in copies:
            copy.start()
            left.append((now, copy.wait_send))

    start(*p_forward(2, 0, 0, "y"), *p_forward(1, 0, 0))

    p_local.start()
    codes_own[...] = jnp.full(codes_own.shape, SLOTS * SLOTS, jnp.int32)
    codes_load.wait()
    codes_own[:, pl.ds(0, SLOTS), pl.ds(0, 16)] = codes_in[...]
    codes_copy.start()
    cols_load.wait()
    pick(0)
    sums[:, 0] = jnp.zeros((16, 2 * BS, BS), jnp.bfloat16)
    p_local.wait()
    p_convert(0, 0, 0, DEPTH)
    pick_copy(0).wait()

    def other_codes():
        codes_copy.wait()
        pick(1)

    def piece_of_p(g, a, b):
        p_wait(g, a, b)
        start(*p_forward(g, a, b, "y" if (g, a) == (2, 0) else "xy"))
        p_convert(a, b, *GROUP[g])

    def across(b):
        start(*p_forward(2, 0, b, "x"))

    def moved(h):
        @pl.when(t >= 4)
        def _():
            a_wait(t, h)
            for way in (1, -1):
                a_copy(t, h, 0, way).start()
            if h == 1:
                sib_copy(t).start()

        for way in (1, -1):
            left.append((now, a_copy(t, h, 0, way).wait_send))
        if h == 1:
            left.append((now, sib_copy(t).wait_send))

    def line():
        @pl.when(core == 1)
        def _():
            pl.semaphore_wait(barrier, 8)
            pl.semaphore_signal(line_ready, inc=1, device_id=sibling, device_id_type=MESH)

        @pl.when(core == 0)
        def _():
            pl.semaphore_wait(line_ready, 1)

        @pl.when(t >= 4)
        def _():
            move_copy.start()
            pass_copy.start()

        @pl.when(t < 4)
        def _():
            for h in range(2):
                for way in (1, -1):
                    a_copy(t, h, 0, way, a_ref.at[pl.ds(h * half, half)]).start()
            a_local.start()
            sib_copy(t, a_ref).start()

    def cross():
        @pl.when(t < 4)
        def _():
            pass_copy.wait_recv()
            cross_copy.start()

    def hop(d, way, h):
        e = source(d, way)
        a_wait(e, h)
        if goes_on(d, way):
            start(a_copy(e, h, d, way))
        if h == 1:
            start(sib_copy(e))

    def add_up(d, way):
        if d == 0:

            @pl.when(t < 4)
            def _():
                a_local.wait()

        e = source(d, way)
        sib_wait(e)
        combine(e)

    def piece_products(d, way):
        if not begun:
            pick_copy(1).wait()
            begun.append(d)
        e = source(d, way)

        @pl.when(e >= 4)
        def _():
            products(1, rows_of(e) - 8, 2)

    steps = {"P": piece_of_p, "M": moved, "H": hop, "C": add_up, "N": cross, "Z": line, "X": across, "O": piece_products}
    for now, (name, *where) in enumerate(ORDER):
        if now == 20:
            other_codes()
        if now == len(ORDER) - 3:
            for began, wait in left:
                if began < now - 20:
                    wait()
            left = [entry for entry in left if entry[0] >= now - 20]
        steps[name](*where)
    products(0, 0, 8)

    for _, wait in left:
        wait()

    @pl.when(t >= 4)
    def _():
        move_copy.wait_send()
        pass_copy.wait_send()

    @pl.when(t < 4)
    def _():
        cross_copy.wait_send()


def shards(a_blocks, p_blocks, out_columns, pair_codes):
    vmem, smem = pltpu.VMEM, pltpu.SMEM
    dma = pltpu.SemaphoreType.DMA
    f32, bf16 = jnp.float32, jnp.bfloat16
    operands = (
        a_blocks.reshape(DEPTH, BS),
        p_blocks.reshape(DEPTH, BS),
        out_columns.T,
        pair_codes.transpose(2, 1, 0),
    )
    product = pl.pallas_call(
        kernel,
        out_shape=jax.ShapeDtypeStruct((8 * SLOTS, BS, BS), f32),
        in_specs=[
            pl.BlockSpec(memory_space=pltpu.HBM),
            pl.BlockSpec(memory_space=pltpu.HBM),
            pl.BlockSpec(memory_space=pltpu.HBM),
            pl.BlockSpec(memory_space=pltpu.HBM),
        ],
        out_specs=pl.BlockSpec(memory_space=vmem),
        scratch_shapes=[
            vmem((16, DEPTH, BS), f32),
            vmem((16, DEPTH, BS), f32),
            vmem((16, DEPTH, 2 * BS), bf16),
            vmem((16, DEPTH, 2 * BS), bf16),
            vmem((16, DEPTH, BS), f32),
            vmem((16, 16, 2 * BS, BS), bf16),
            smem((SLOTS, 16), jnp.int32),
            vmem((MP, SLOTS, 16), jnp.int32),
            vmem((MP, 8, BS), jnp.int32),
            vmem((MP, 8, BS), jnp.int32),
            vmem((SLOTS, 8, BS), jnp.int32),
            vmem((SLOTS, 8, BS), jnp.int32),
            smem((SLOTS, 8, BS), jnp.int32),
            smem((SLOTS, 8, BS), jnp.int32),
            vmem((DEPTH // 2, BS), f32),
            dma((2, 4, 8)),
            dma((2, 4, 8)),
            dma((2, 8)),
            dma((2, 2, 4)),
            dma((8,)),
            dma((8,)),
            dma((2,)),
            dma((2,)),
            dma((2,)),
            dma((6,)),
            pltpu.SemaphoreType.REGULAR,
            pltpu.SemaphoreType.REGULAR,
        ],
        compiler_params=pltpu.CompilerParams(
            collective_id=0, has_side_effects=True, vmem_limit_bytes=44 * 2**20
        ),
        cost_estimate=pl.CostEstimate(flops=4 * 10**9, bytes_accessed=5 * 2**20, transcendentals=0),
    )(*(pltpu.with_memory_space_constraint(operand, pltpu.HBM) for operand in operands))
    return product.reshape(8, SLOTS, BS, BS)


def solution(mesh):
    return jax.shard_map(
        shards,
        mesh=mesh,
        in_specs=(
            P(("row", "col"), "layer", None, None),
            P(("row", "col"), "layer", None, None),
            P("row", "col"),
            P("row", "col", "layer"),
        ),
        out_specs=P(("row", "layer"), "col", None, None),
        check_vma=False,
    )
```

```python
import jax
import jax.numpy as jnp
from jax import lax
from jax.experimental import pallas as pl
from jax.experimental.pallas import tpu as pltpu
from jax.sharding import PartitionSpec as P

MESH = pl.DeviceIdType.MESH
BS = 128
SLOTS = 4
DEPTH = SLOTS * BS
MP = 7
NX, NY, NZ = 4, 8, 8
R1 = 208
GROUP = {1: (0, R1), 2: (R1, DEPTH - R1)}
ORDER = (
    ("X", 0), ("Z",), ("P", 1, 1, 0), ("P", 2, 0, 1), ("X", 1), ("P", 1, 0, -1), ("P", 2, 0, -1), ("X", -1),
    ("P", 1, -1, 0), ("N",), ("P", 1, 0, 1), ("P", 2, 0, 2), ("X", 2), ("P", 2, 0, -2), ("X", -2), ("P", 1, 1, 1),
    ("P", 1, 0, -2), ("P", 1, 2, 0), ("M", 0), ("P", 2, -1, 0), ("P", 2, -1, 1), ("P", 2, 1, 1), ("P", 1, -1, 1),
    ("P", 2, 1, 0), ("M", 1), ("P", 1, 0, 2), ("H", 1, -1, 0), ("P", 1, 1, -1), ("H", 1, 1, 0), ("P", 2, 1, -2),
    ("H", 1, 1, 1), ("P", 2, -1, -1), ("P", 1, 1, 2), ("P", 2, 1, -1), ("P", 2, 0, 3), ("X", 3), ("P", 1, 0, -3),
    ("P", 2, 0, -3), ("X", -3), ("H", 2, 1, 0), ("P", 1, -1, -1), ("H", 1, -1, 1), ("P", 1, 2, -1), ("H", 2, 1, 1),
    ("P", 1, 1, -2), ("C", 1, 1), ("H", 3, 1, 0), ("P", 1, 2, 1), ("C", 0, 1), ("H", 2, -1, 0), ("P", 1, 0, 3),
    ("P", 2, -1, 2), ("P", 1, -1, 2), ("H", 2, -1, 1), ("C", 1, -1), ("H", 3, 1, 1), ("C", 2, 1), ("P", 1, 1, 3),
    ("P", 2, 0, 4), ("X", 4), ("C", 2, -1), ("P", 2, 2, 1), ("P", 2, 2, -1), ("P", 1, -1, -2), ("H", 4, 1, 0),
    ("P", 2, 1, 2), ("P", 2, -1, -2), ("P", 1, 2, 2), ("P", 2, -1, 3), ("P", 1, -1, 3), ("P", 1, 1, -3),
    ("P", 2, 2, 0), ("P", 2, 1, -3), ("P", 1, 1, 4), ("P", 2, 2, -2), ("H", 3, -1, 0), ("H", 4, 1, 1),
    ("P", 1, 2, -2), ("H", 3, -1, 1), ("C", 3, -1), ("P", 1, -1, -3), ("P", 2, 1, 4), ("P", 2, 1, 3), ("C", 3, 1),
    ("P", 1, 2, 3), ("C", 4, 1), ("P", 2, -1, -3), ("P", 2, 2, 2), ("P", 1, -1, 4), ("P", 2, -1, 4), ("O", 1, -1),
    ("O", 3, -1), ("O", 1, 1), ("O", 2, 1), ("O", 2, -1), ("O", 0, 1), ("O", 3, 1), ("P", 1, 2, -3), ("O", 4, 1),
    ("P", 2, 2, 3), ("P", 2, 2, 4), ("P", 1, 0, 4), ("P", 2, 2, -3), ("P", 1, 2, 4),
)


def onward(g, a, b):
    out = []
    if g == 1:
        if b == 0:
            if a == 0:
                out += [(1, 0, "x", 1), (-1, 0, "x", -1)]
            if a == 1:
                out += [(2, 0, "x", 1)]
            out += [(a, 1, "y", 1), (a, -1, "y", -1)]
        elif 0 < b < 4:
            out += [(a, b + 1, "y", 1)]
        elif -3 < b < 0:
            out += [(a, b - 1, "y", -1)]
    else:
        if a == 0:
            if b == 0:
                out += [(0, 1, "y", 1), (0, -1, "y", -1)]
            elif 0 < b < 4:
                out += [(0, b + 1, "y", 1)]
            elif -3 < b < 0:
                out += [(0, b - 1, "y", -1)]
            out += [(1, b, "x", 1), (-1, b, "x", -1)]
        elif a == 1:
            out += [(2, b, "x", 1)]
    return out


def kernel(
    a_ref, p_ref, cols_ref, codes_ref, out_ref,
    p_own, p_opp, ps_own, ps_opp, a_all, sums, cols, codes_in, codes_own, codes_opp,
    picks_own, picks_opp, picks_smem_own, picks_smem_opp,
    passing, p_recv, p_send, a_recv, a_send, sib_recv, sib_send, move_send, pass_sem, codes_sem, local_sem, plane_ready, line_ready,
):
    row, col, layer = lax.axis_index("row"), lax.axis_index("col"), lax.axis_index("layer")
    y, z, core = lax.rem(row, NY), col // 2, lax.rem(col, 2)
    x = (row // NY) * 2 + layer
    turn = 1 - 2 * core
    t = lax.rem(z + 2 * NZ - 4 * layer, NZ)
    q_me = row

    def device(x_, y_, z_, core_):
        return ((x_ // 2) * NY + y_, z_ * 2 + core_, lax.rem(x_, 2))

    def along(axis, way):
        if axis == "x":
            return device(lax.rem(x + NX + turn * way, NX), y, z, core)
        if axis == "y":
            return device(x, lax.rem(y + NY + turn * way, NY), z, core)
        return device(x, y, lax.rem(z + NZ + turn * way, NZ), core)

    sibling = device(x, y, z, 1 - core)
    partner = (row, col, 1 - layer)
    mover = (row, (NZ - 1 - z) * 2 + core, 1 - layer)
    opposite = (row, (NZ - 1 - z) * 2 + core, layer)

    codes_load = pltpu.make_async_copy(codes_ref, codes_in, local_sem.at[4])
    cols_load = pltpu.make_async_copy(cols_ref, cols, local_sem.at[5])
    codes_load.start()
    cols_load.start()

    barrier = pltpu.get_barrier_semaphore()
    for axis in "xy":
        for way in (1, -1):
            row_, _, layer_ = along(axis, way)
            pl.semaphore_signal(barrier, inc=1, device_id=(row_, z * 2, layer_), device_id_type=MESH)
    for row_, col_, layer_ in (along("z", 1), along("z", -1), mover, opposite):
        pl.semaphore_signal(barrier, inc=1, device_id=(row_, (col_ // 2) * 2 + 1, layer_), device_id_type=MESH)

    @pl.when(core == 0)
    def _():
        pl.semaphore_wait(barrier, 9)
        pl.semaphore_signal(plane_ready, inc=1, device_id=sibling, device_id_type=MESH)

    @pl.when(core == 1)
    def _():
        pl.semaphore_signal(barrier, inc=1, device_id=sibling, device_id_type=MESH)
        pl.semaphore_wait(plane_ready, 1)

    p_land = (p_own, p_opp)
    p_split = (ps_own, ps_opp)
    picks = (picks_own, picks_opp)
    picks_smem = (picks_smem_own, picks_smem_opp)
    codes_land = (codes_own, codes_opp)

    def p_slot(a, b):
        x0 = lax.rem(x + 2 * NX - turn * a, NX)
        y0 = lax.rem(y + 2 * NY - turn * b, NY)
        return (x0 // 2) * NY + y0


    def p_piece(g, a, b):
        lo, size = GROUP[g]
        return p_land[a % 2].at[p_slot(a, b), pl.ds(lo, size)]

    def p_forward(g, a, b, axes="xy"):
        lo, size = GROUP[g]
        src = p_ref.at[pl.ds(lo, size)] if (a, b) == (0, 0) else p_piece(g, a, b)
        copies = []
        for a2, b2, axis, way in onward(g, a, b):
            if axis not in axes:
                continue
            copies.append(
                pltpu.make_async_remote_copy(
                    src_ref=src,
                    dst_ref=p_land[a2 % 2].at[p_slot(a, b), pl.ds(lo, size)],
                    send_sem=p_send.at[g - 1, a2 + 1, b2 + 3],
                    recv_sem=p_recv.at[g - 1, a2 + 1, b2 + 3],
                    device_id=along(axis, way),
                    device_id_type=MESH,
                )
            )
        return copies

    def p_wait(g, a, b):
        here = p_piece(g, a, b)
        pltpu.make_async_remote_copy(
            src_ref=here,
            dst_ref=here,
            send_sem=p_send.at[g - 1, a + 1, b + 3],
            recv_sem=p_recv.at[g - 1, a + 1, b + 3],
            device_id=along("x", 1),
            device_id_type=MESH,
        ).wait_recv()

    def p_convert(a, b, lo, size):
        q = p_slot(a, b)
        value = p_land[a % 2][q, pl.ds(lo, size), :]
        high = value.astype(jnp.bfloat16)
        low = (value - high.astype(jnp.float32)).astype(jnp.bfloat16)
        p_split[a % 2][q, pl.ds(lo, size), pl.ds(0, BS)] = high
        p_split[a % 2][q, pl.ds(lo, size), pl.ds(BS, BS)] = low

    half = DEPTH // 2

    def rows_of(e):
        return jnp.where(e < 4, 2 * e, 8 + 2 * (7 - e))

    def a_half(e, h):
        return a_all.at[rows_of(e) + core, pl.ds(h * half, half)]

    def a_copy(e, h, d, way, src=None):
        return pltpu.make_async_remote_copy(
            src_ref=a_half(e, h) if src is None else src,
            dst_ref=a_half(e, h),
            send_sem=a_send.at[h, (1 - way) // 2, d],
            recv_sem=a_recv.at[h, e],
            device_id=along("z", way),
            device_id_type=MESH,
        )

    def a_wait(e, h):
        a_copy(e, h, 0, 1).wait_recv()

    def sib_copy(e, src=None):
        here = a_all.at[rows_of(e) + core]
        return pltpu.make_async_remote_copy(
            src_ref=here if src is None else src,
            dst_ref=here,
            send_sem=sib_send.at[e],
            recv_sem=sib_recv.at[e],
            device_id=sibling,
            device_id_type=MESH,
        )

    def sib_wait(e):
        there = a_all.at[rows_of(e) + 1 - core]
        pltpu.make_async_remote_copy(
            src_ref=there,
            dst_ref=there,
            send_sem=sib_send.at[e],
            recv_sem=sib_recv.at[e],
            device_id=sibling,
            device_id_type=MESH,
        ).wait_recv()

    move_copy = pltpu.make_async_remote_copy(
        src_ref=a_ref.at[pl.ds(0, half)],
        dst_ref=a_half(11 - t, 0),
        send_sem=move_send.at[0],
        recv_sem=a_recv.at[0, 11 - t],
        device_id=mover,
        device_id_type=MESH,
    )
    pass_copy = pltpu.make_async_remote_copy(
        src_ref=a_ref.at[pl.ds(half, half)],
        dst_ref=passing,
        send_sem=pass_sem.at[0],
        recv_sem=pass_sem.at[1],
        device_id=opposite,
        device_id_type=MESH,
    )
    cross_copy = pltpu.make_async_remote_copy(
        src_ref=passing,
        dst_ref=a_half(t + 4, 1),
        send_sem=move_send.at[1],
        recv_sem=a_recv.at[1, t + 4],
        device_id=partner,
        device_id_type=MESH,
    )

    def source(d, way):
        return lax.rem(t + 2 * NZ - turn * way * d, NZ)

    def goes_on(d, way):
        return d < (4 if way == 1 else 3)

    codes_copy = pltpu.make_async_remote_copy(
        src_ref=codes_own,
        dst_ref=codes_opp,
        send_sem=codes_sem.at[0],
        recv_sem=codes_sem.at[1],
        device_id=partner,
        device_id_type=MESH,
    )

    def pick_copy(which):
        return pltpu.make_async_copy(picks[which], picks_smem[which], local_sem.at[2 + which])

    def pick(which):
        codes = [codes_land[which][m] for m in range(MP)]
        for p in range(SLOTS):
            total = jnp.zeros((8, BS), jnp.int32)
            for code in codes:
                for a in range(SLOTS):
                    total += jnp.where(code == a * SLOTS + p, 1 << a, 0)
            picks[which][p] = total
        pick_copy(which).start()

    def combine(e):
        def step(i, carry):
            r = rows_of(e) + i
            strip = 16
            for k in range(BS // strip):
                total = {0: None}
                for n in range(1, 16):
                    a = n.bit_length() - 1
                    part = a_all[r, pl.ds(a * BS + k * strip, strip), :] if n == 1 << a else None
                    total[n] = part if n == 1 << a else total[n - (1 << a)] + total[1 << a]
                    high = total[n].astype(jnp.bfloat16)
                    low = (total[n] - high.astype(jnp.float32)).astype(jnp.bfloat16)
                    sums[r, n, pl.ds(k * strip, strip), :] = high
                    sums[r, n, pl.ds(BS + k * strip, strip), :] = low
            return carry

        lax.fori_loop(0, 2, step, 0)

    def products(which, first, count):
        def step(i, carry):
            r = first + i
            at = 8 * layer + r
            for o in range(SLOTS):
                q = cols[o, at]
                left = jnp.concatenate([sums[8 * which + r, picks_smem[which][p, o, at]] for p in range(SLOTS)], axis=1)
                four = jnp.dot(left, p_split[which][q], preferred_element_type=jnp.float32)
                value = (four[BS:, BS:] + four[:BS, BS:] + four[BS:, :BS]) + four[:BS, :BS]
                where = r * SLOTS + o
                out_ref[where] = value if which == 1 else out_ref[where] + value
            return carry

        lax.fori_loop(0, count, step, 0)

    p_local = pltpu.make_async_copy(p_ref, p_own.at[q_me], local_sem.at[0])
    a_local = pltpu.make_async_copy(a_ref, a_all.at[rows_of(lax.rem(t, 4)) + core], local_sem.at[1])

    begun = []
    left = []
    now = -1

    def start(*copies):
        for copy in copies:
            copy.start()
            left.append((now, copy.wait_send))

    start(*p_forward(2, 0, 0, "y"), *p_forward(1, 0, 0))

    p_local.start()
    codes_own[...] = jnp.full(codes_own.shape, SLOTS * SLOTS, jnp.int32)
    codes_load.wait()
    codes_own[:, pl.ds(0, SLOTS), pl.ds(0, 16)] = codes_in[...]
    codes_copy.start()
    cols_load.wait()
    pick(0)
    sums[:, 0] = jnp.zeros((16, 2 * BS, BS), jnp.bfloat16)
    p_local.wait()
    p_convert(0, 0, 0, DEPTH)
    pick_copy(0).wait()

    def other_codes():
        codes_copy.wait()
        pick(1)

    def piece_of_p(g, a, b):
        p_wait(g, a, b)
        start(*p_forward(g, a, b, "y" if (g, a) == (2, 0) else "xy"))
        p_convert(a, b, *GROUP[g])

    def across(b):
        start(*p_forward(2, 0, b, "x"))

    def moved(h):
        @pl.when(t >= 4)
        def _():
            a_wait(t, h)
            for way in (1, -1):
                a_copy(t, h, 0, way).start()
            if h == 1:
                sib_copy(t).start()

        for way in (1, -1):
            left.append((now, a_copy(t, h, 0, way).wait_send))
        if h == 1:
            left.append((now, sib_copy(t).wait_send))

    def line():
        @pl.when(core == 1)
        def _():
            pl.semaphore_wait(barrier, 8)
            pl.semaphore_signal(line_ready, inc=1, device_id=sibling, device_id_type=MESH)

        @pl.when(core == 0)
        def _():
            pl.semaphore_wait(line_ready, 1)

        @pl.when(t >= 4)
        def _():
            move_copy.start()
            pass_copy.start()

        @pl.when(t < 4)
        def _():
            for h in range(2):
                for way in (1, -1):
                    a_copy(t, h, 0, way, a_ref.at[pl.ds(h * half, half)]).start()
            a_local.start()
            sib_copy(t, a_ref).start()

    def cross():
        @pl.when(t < 4)
        def _():
            pass_copy.wait_recv()
            cross_copy.start()

    def hop(d, way, h):
        e = source(d, way)
        a_wait(e, h)
        if goes_on(d, way):
            start(a_copy(e, h, d, way))
        if h == 1:
            start(sib_copy(e))

    def add_up(d, way):
        if d == 0:

            @pl.when(t < 4)
            def _():
                a_local.wait()

        e = source(d, way)
        sib_wait(e)
        combine(e)

    def piece_products(d, way):
        if not begun:
            pick_copy(1).wait()
            begun.append(d)
        e = source(d, way)

        @pl.when(e >= 4)
        def _():
            products(1, rows_of(e) - 8, 2)

    steps = {"P": piece_of_p, "M": moved, "H": hop, "C": add_up, "N": cross, "Z": line, "X": across, "O": piece_products}
    for now, (name, *where) in enumerate(ORDER):
        if now == 20:
            other_codes()
        if now == len(ORDER) - 3:
            for began, wait in left:
                if began < now - 20:
                    wait()
            left = [entry for entry in left if entry[0] >= now - 20]
        steps[name](*where)
    products(0, 0, 8)

    for _, wait in left:
        wait()

    @pl.when(t >= 4)
    def _():
        move_copy.wait_send()
        pass_copy.wait_send()

    @pl.when(t < 4)
    def _():
        cross_copy.wait_send()


def shards(a_blocks, p_blocks, out_columns, pair_codes):
    vmem, smem = pltpu.VMEM, pltpu.SMEM
    dma = pltpu.SemaphoreType.DMA
    f32, bf16 = jnp.float32, jnp.bfloat16
    operands = (
        a_blocks.reshape(DEPTH, BS),
        p_blocks.reshape(DEPTH, BS),
        out_columns.T,
        pair_codes.transpose(2, 1, 0),
    )
    product = pl.pallas_call(
        kernel,
        out_shape=jax.ShapeDtypeStruct((8 * SLOTS, BS, BS), f32),
        in_specs=[
            pl.BlockSpec(memory_space=pltpu.HBM),
            pl.BlockSpec(memory_space=pltpu.HBM),
            pl.BlockSpec(memory_space=pltpu.HBM),
            pl.BlockSpec(memory_space=pltpu.HBM),
        ],
        out_specs=pl.BlockSpec(memory_space=vmem),
        scratch_shapes=[
            vmem((16, DEPTH, BS), f32),
            vmem((16, DEPTH, BS), f32),
            vmem((16, DEPTH, 2 * BS), bf16),
            vmem((16, DEPTH, 2 * BS), bf16),
            vmem((16, DEPTH, BS), f32),
            vmem((16, 16, 2 * BS, BS), bf16),
            smem((SLOTS, 16), jnp.int32),
            vmem((MP, SLOTS, 16), jnp.int32),
            vmem((MP, 8, BS), jnp.int32),
            vmem((MP, 8, BS), jnp.int32),
            vmem((SLOTS, 8, BS), jnp.int32),
            vmem((SLOTS, 8, BS), jnp.int32),
            smem((SLOTS, 8, BS), jnp.int32),
            smem((SLOTS, 8, BS), jnp.int32),
            vmem((DEPTH // 2, BS), f32),
            dma((2, 4, 8)),
            dma((2, 4, 8)),
            dma((2, 8)),
            dma((2, 2, 4)),
            dma((8,)),
            dma((8,)),
            dma((2,)),
            dma((2,)),
            dma((2,)),
            dma((6,)),
            pltpu.SemaphoreType.REGULAR,
            pltpu.SemaphoreType.REGULAR,
        ],
        compiler_params=pltpu.CompilerParams(
            collective_id=0, has_side_effects=True, vmem_limit_bytes=44 * 2**20
        ),
        cost_estimate=pl.CostEstimate(flops=4 * 10**9, bytes_accessed=5 * 2**20, transcendentals=0),
    )(*(pltpu.with_memory_space_constraint(operand, pltpu.HBM) for operand in operands))
    return product.reshape(8, SLOTS, BS, BS)


def solution(mesh):
    return jax.shard_map(
        shards,
        mesh=mesh,
        in_specs=(
            P(("row", "col"), "layer", None, None),
            P(("row", "col"), "layer", None, None),
            P("row", "col"),
            P("row", "col", "layer"),
        ),
        out_specs=P(("row", "layer"), "col", None, None),
        check_vma=False,
    )
```
